32 devices in a mesh: wide: 16 (over z, y, x), narrow: 2 (over core).
Axes of the slice: x: 2, y: 2, z: 4, core: 2. Of those that a mesh axis runs over, the one named last changes fastest.
Arguments:
- hidden_in: bfloat16 [2, 16, 512, 1152], P(None, 'wide', 'narrow'), may hold values from -6 to 6
- cond_vec: bfloat16 [2, 16, 8, 1152], P(None, 'wide'), may hold values from -6 to 6
- seg_ids: int32 [2, 16, 512], P(None, 'wide'), may hold values from 0 to 6, as said below
- grid_pos: int32 [2, 2, 16, 512], P(None, None, 'wide', 'narrow'), may hold values from 0 to 63, as said below
- out_grad: bfloat16 [2, 16, 512, 1152], P(None, 'wide', 'narrow'), may hold values from -6 to 6
- w_ada: bfloat16 [1152, 6912], P(('wide', 'narrow')), may hold values from -0.1875 to 0.1875
- b_ada: bfloat16 [6912], P(('wide', 'narrow')), may hold values from -3 to 3
- w_qkv: bfloat16 [1152, 3456], P(('wide', 'narrow')), may hold values from -0.1875 to 0.1875
- b_qkv: bfloat16 [3456], P(('wide', 'narrow')), may hold values from -2 to 2
- w_out: bfloat16 [1152, 1152], P(('wide', 'narrow')), may hold values from -1.5 to 1.5
- b_out: bfloat16 [1152], P(('wide', 'narrow')), may hold values from -2 to 2
- w_gate: bfloat16 [1152, 3072], P('wide', 'narrow'), may hold values from -0.1875 to 0.1875
- w_up: bfloat16 [1152, 3072], P('wide', 'narrow'), may hold values from -0.1875 to 0.1875
- w_down: bfloat16 [3072, 1152], P('narrow', 'wide'), may hold values from -0.15625 to 0.15625
Outputs:
- output: float32 [2, 16, 512, 1152], P(None, 'wide', 'narrow')
- in_grad: float32 [2, 16, 512, 1152], P(None, 'wide', 'narrow')
- grad_w_ada: float32 [1152, 6912], P(('wide', 'narrow'))
- grad_b_ada: float32 [6912], P(('wide', 'narrow'))
- grad_w_qkv: float32 [1152, 3456], P(('wide', 'narrow'))
- grad_b_qkv: float32 [3456], P(('wide', 'narrow'))
- grad_w_out: float32 [1152, 1152], P(('wide', 'narrow'))
- grad_b_out: float32 [1152], P(('wide', 'narrow'))
- grad_w_gate: float32 [1152, 3072], P('wide', 'narrow')
- grad_w_up: float32 [1152, 3072], P('wide', 'narrow')
- grad_w_down: float32 [3072, 1152], P('narrow', 'wide')
The draws below stay inside these ranges and needn't reach their ends.
Inputs may be any that keep to these rules, and one draw needn't show every extreme that they name: `seg_ids`: within each buffer ids start at 0 and never fall; each image holds at least 64 and at most 255 tokens, so a buffer has at most 7 images, and the first buffer has exactly 7; in every buffer one image holds both token 255 and token 256. `grid_pos`: Row-major places within each image: row = place // width, column = place % width, for an image width of 4 to 16 drawn per image; the second buffer holds an image of width 16 and one of 255 tokens of width 4.
All inputs are finite; a program needn't handle non-finite values.
Results may differ from the reference program's by a relative error of at most 0.015.
The reference program's roundings to bfloat16 on the way count: a program that leaves them out, or rounds other values in their place, can miss the bound.
Values may be sent and summed in bfloat16 or wider, within the bound.
A program may use at most 256 MiB of HBM per device.

```python
import jax
import jax.numpy as jnp
from jax import lax

D = 1152
HEADS = 16
HEAD = 72
FF = 3072
MB = 2
BLOCK = 32
SEGS = 8
BUF_TOK = 512
BUFFERS = 16


def layout(key):
    count = MB * BUFFERS
    keys = jax.random.split(key, 3)
    extra = jax.random.randint(keys[0], (count, 1), 1, BLOCK)
    spans = jax.random.randint(keys[1], (count, SEGS), 2, 7)
    widths = jax.random.randint(keys[2], (count, SEGS), 4, 17)
    spans = spans.at[0].set(2)
    spans = spans.at[1].set(6)
    spans = spans.at[1, 0].set(2)
    extra = extra.at[1, 0].set(1)
    widths = widths.at[1].set(4)
    widths = widths.at[1, 1].set(16)
    ends = jnp.cumsum(spans, axis=1)
    cuts = jnp.where(ends <= 13, extra + BLOCK * ends, BUF_TOK + 1)
    place = jnp.arange(BUF_TOK, dtype=jnp.int32)[None, :]
    segs = jnp.sum((place[:, :, None] >= cuts[:, None, :]).astype(jnp.int32), axis=2)
    starts = jnp.concatenate([jnp.zeros((count, 1), jnp.int32), cuts[:, :-1]], axis=1)
    picked = segs[:, :, None] == jnp.arange(SEGS, dtype=jnp.int32)[None, None, :]
    start_tok = jnp.sum(jnp.where(picked, starts[:, None, :], 0), axis=2)
    width_tok = jnp.sum(jnp.where(picked, widths[:, None, :], 0), axis=2)
    offset = place - start_tok
    return (segs, offset // width_tok, offset % width_tok)


def draw_seg_ids(key, part):
    segs, rows, cols = layout(key)
    return segs.reshape(MB, BUFFERS, BUF_TOK).astype(jnp.int32)


def draw_grid_pos(key, part):
    segs, rows, cols = layout(key)
    return jnp.stack([rows, cols]).reshape(2, MB, BUFFERS, BUF_TOK).astype(jnp.int32)


def levels(stream_key, shape, cuts, smallest, top_value):
    def one(position, parts):
        heights = jax.random.uniform(jax.random.fold_in(jax.random.fold_in(stream_key, 6), position), (parts,), jnp.float32, smallest / len(cuts), top_value / len(cuts))
        return jnp.repeat(jnp.exp(heights), shape[position] // parts).reshape((-1,) + (1,) * (len(shape) - position - 1))

    factor_of = one(*cuts[0])
    for cut in cuts[1:]:
        factor_of = factor_of * one(*cut)
    return factor_of


def gaussian(own_key, extent, scale, bound, cuts=(), held_as=jnp.bfloat16):
    values = scale * jax.random.normal(own_key, extent, jnp.float32)
    if cuts:
        values = values * levels(own_key, extent, cuts, -0.22, 0.18)
    return jnp.clip(values, -bound, bound).astype(held_as)


def setup_inputs(seed: int = 0) -> dict:
    arg_keys = jax.random.split(jax.random.key(seed), 15)
    hidden_in = gaussian(arg_keys[0], (MB, BUFFERS, BUF_TOK, D), 1.0, 6.0, ((1, 16), (2, 2)))
    cond_vec = gaussian(arg_keys[1], (MB, BUFFERS, SEGS, D), 1.0, 6.0, ((1, 16),))
    seg_ids = draw_seg_ids(jax.random.fold_in(arg_keys[14], 71), 0)
    grid_pos = draw_grid_pos(jax.random.fold_in(arg_keys[14], 71), 0)
    out_grad = gaussian(arg_keys[4], (MB, BUFFERS, BUF_TOK, D), 1.0, 6.0, ((1, 16), (2, 2)))
    w_ada = gaussian(arg_keys[5], (D, 6 * D), D ** -0.5, 0.1875, ((0, 32),))
    b_ada = gaussian(arg_keys[6], (6 * D,), 0.5, 3.0, ((0, 32),))
    w_qkv = gaussian(arg_keys[7], (D, 3 * D), D ** -0.5, 0.1875, ((0, 32),))
    b_qkv = gaussian(arg_keys[8], (3 * D,), 0.3, 2.0, ((0, 32),))
    w_out = gaussian(arg_keys[9], (D, D), (max(D // 64, 1)) ** -0.5, 1.5, ((0, 32),))
    b_out = gaussian(arg_keys[10], (D,), 0.3, 2.0, ((0, 32),))
    w_gate = gaussian(arg_keys[11], (D, FF), D ** -0.5, 0.1875, ((0, 16), (1, 2)))
    w_up = gaussian(arg_keys[12], (D, FF), D ** -0.5, 0.1875, ((0, 16), (1, 2)))
    w_down = gaussian(arg_keys[13], (FF, D), (FF // 2) ** -0.5, 0.15625, ((0, 2), (1, 16)))
    return dict(hidden_in=hidden_in, cond_vec=cond_vec, seg_ids=seg_ids, grid_pos=grid_pos, out_grad=out_grad, w_ada=w_ada, b_ada=b_ada, w_qkv=w_qkv, b_qkv=b_qkv, w_out=w_out, b_out=b_out, w_gate=w_gate, w_up=w_up, w_down=w_down)


@jax.custom_vjp
def low(v):
    return lax.optimization_barrier(v.astype(jnp.bfloat16)).astype(jnp.float32)

@jax.custom_vjp
def low_back(v):
    return v

def low_keep(v):
    return (low(v), None)

def low_pass(kept, grad):
    return (grad,)

def back_keep(v):
    return (v, None)

def back_low(kept, grad):
    return (low(grad),)
low.defvjp(low_keep, low_pass)
low_back.defvjp(back_keep, back_low)

def layer_norm(values):
    centred = values - lax.optimization_barrier(jnp.mean(values, axis=-1, keepdims=True))
    return centred * lax.rsqrt(lax.optimization_barrier(jnp.mean(centred * centred, axis=-1, keepdims=True)) + 1e-06)

def angle_tables(rows, cols, head):
    quarter = head // 4
    freq = 10000.0 ** (-jnp.arange(quarter, dtype=jnp.float32) / quarter)
    row_angle = rows.astype(jnp.float32)[:, None, None] * freq
    col_angle = cols.astype(jnp.float32)[:, None, None] * freq
    return (jnp.cos(row_angle), jnp.sin(row_angle), jnp.cos(col_angle), jnp.sin(col_angle))

def rotate(values, cos_row, sin_row, cos_col, sin_col, sign):
    first, second, third, fourth = jnp.split(values, 4, axis=-1)
    return jnp.concatenate([first * cos_row - sign * second * sin_row, second * cos_row + sign * first * sin_row, third * cos_col - sign * fourth * sin_col, fourth * cos_col + sign * third * sin_col], axis=-1)

def buffer_forward(tokens, cond_rows, segs, rows, cols, ada_w, ada_b, qkv_w, qkv_b, out_w, out_b, gate_w, up_w, down_w):
    highest = lax.Precision.HIGHEST
    width = tokens.shape[-1]
    count = tokens.shape[0]
    cond_low = low(jax.nn.silu(cond_rows))
    modul = jnp.dot(cond_low, ada_w, precision=highest) + ada_b
    per_tok = modul[segs]
    shift1, scale1, gate1, shift2, scale2, gate2 = jnp.split(per_tok, 6, axis=1)
    normed1 = layer_norm(tokens)
    a_low = low(normed1 * (1.0 + scale1) + shift1)
    qkv = low_back(jnp.dot(a_low, qkv_w, precision=highest) + qkv_b)
    tables = angle_tables(rows, cols, HEAD)
    query = low(rotate(qkv[:, :width].reshape(count, HEADS, HEAD), *tables, 1.0))
    keys = low(rotate(qkv[:, width:2 * width].reshape(count, HEADS, HEAD), *tables, 1.0))
    values = low(qkv[:, 2 * width:].reshape(count, HEADS, HEAD))
    scores = low_back(jnp.einsum('qhd,khd->hqk', query, keys, precision=highest) * HEAD ** (-0.5))
    same = segs[:, None] == segs[None, :]
    scores = jnp.where(same[None], scores, -1e+30)
    probs = low(jax.nn.softmax(scores, axis=-1))
    attended = jnp.einsum('hqk,khd->qhd', probs, values, precision=highest).reshape(count, width)
    attended = low_back(low(attended))
    branch = low_back(jnp.dot(attended, out_w, precision=highest) + out_b)
    mixed = tokens + gate1 * branch
    normed2 = layer_norm(mixed)
    c_low = low(normed2 * (1.0 + scale2) + shift2)
    gate = low_back(jnp.dot(c_low, gate_w, precision=highest))
    up = low_back(jnp.dot(c_low, up_w, precision=highest))
    hid_low = low(jax.nn.silu(gate) * up)
    mlp = low_back(jnp.dot(hid_low, down_w, precision=highest))
    return mixed + gate2 * mlp

def reference(hidden_in, cond_vec, seg_ids, grid_pos, out_grad, w_ada, b_ada, w_qkv, b_qkv, w_out, b_out, w_gate, w_up, w_down):
    weights = tuple((w.astype(jnp.float32) for w in (w_ada, b_ada, w_qkv, b_qkv, w_out, b_out, w_gate, w_up, w_down)))
    count = MB * BUFFERS
    pieces = (hidden_in.reshape(count, BUF_TOK, D).astype(jnp.float32), cond_vec.reshape(count, SEGS, D).astype(jnp.float32), seg_ids.reshape(count, BUF_TOK).astype(jnp.int32), grid_pos[0].reshape(count, BUF_TOK).astype(jnp.int32), grid_pos[1].reshape(count, BUF_TOK).astype(jnp.int32), out_grad.reshape(count, BUF_TOK, D).astype(jnp.float32))

    def step(totals, piece):
        tokens, cond_rows, segs, rows, cols, cotangent = piece

        def forward(tok, *params):
            return buffer_forward(tok, cond_rows, segs, rows, cols, *params)
        result, pullback = jax.vjp(forward, tokens, *weights)
        grads = pullback(cotangent)
        totals = tuple((total + grad for total, grad in zip(totals, grads[1:])))
        return (totals, (result, grads[0]))
    zeros = tuple((jnp.zeros(w.shape, jnp.float32) for w in weights))
    totals, (results, in_grads) = lax.scan(step, zeros, pieces)
    output = results.reshape(MB, BUFFERS, BUF_TOK, D)
    in_grad = in_grads.reshape(MB, BUFFERS, BUF_TOK, D)
    return (output, in_grad, totals[0], totals[1], totals[2], totals[3], totals[4], totals[5], totals[6], totals[7], totals[8])
```

```python
import functools

import jax
import jax.numpy as jnp
from jax import lax
from jax.experimental import pallas as pl
from jax.experimental.pallas import tpu as pltpu
from jax.sharding import PartitionSpec as P

HEADS = 16
HEAD = 72
PAD = 128
F32 = jnp.float32
BF16 = jnp.bfloat16
HIGHEST = lax.Precision.HIGHEST
VMEM = 56 * 2**20


def dot(a, b):
    return jnp.dot(a, b, preferred_element_type=F32)


def dot_nt(a, b):
    return lax.dot_general(a, b, (((1,), (1,)), ((), ())), preferred_element_type=F32)


def dot_tn(a, b):
    return lax.dot_general(a, b, (((0,), (0,)), ((), ())), preferred_element_type=F32)


def wide_axes(count):
    if count == 16:
        lengths = (4, 2, 2)
    elif count == 64:
        lengths = (4, 4, 4)
    else:
        lengths = (2,) * (count.bit_length() - 1)
    axes, stride = [], count
    for length in lengths:
        stride //= length
        axes.append((stride, length))
    return axes


def push(x, count, mask):
    return lax.ppermute(x, "wide", [(i, i ^ mask) for i in range(count)])


def swap(x):
    return lax.ppermute(x, "narrow", [(0, 1), (1, 0)])


def gather_slots(own, count, order):
    parts, masks = [own[None]], [[0]]
    for stride, length in order:
        have = parts[0] if len(parts) == 1 else jnp.concatenate(parts, axis=0)
        seen = sum(masks, [])
        parts, masks = [have], [seen]
        for step in range(1, length):
            parts.append(push(have, count, step * stride))
            masks.append([m ^ (step * stride) for m in seen])
    return parts, masks


def assemble(pieces, count, rows, cols):
    out = None
    me = lax.axis_index("wide")
    for array, masks, first in pieces:
        width = array.shape[2]
        places = me ^ jnp.array(masks, jnp.int32)

        def body(place_ref, in_ref, *refs):
            refs[-1][...] = in_ref[...]

        held = [] if out is None else [out]
        out = pl.pallas_call(
            body,
            out_shape=jax.ShapeDtypeStruct((count, rows, cols), BF16),
            grid_spec=pltpu.PrefetchScalarGridSpec(
                num_scalar_prefetch=1,
                grid=(len(masks),),
                in_specs=[pl.BlockSpec((1, rows, width), lambda s, p: (s, 0, 0))]
                + [pl.BlockSpec(memory_space=pl.ANY)] * len(held),
                out_specs=pl.BlockSpec((1, rows, width), lambda s, p, c=first // width: (p[s], 0, c)),
            ),
            input_output_aliases={2: 0} if held else {},
            cost_estimate=pl.CostEstimate(
                flops=0, bytes_accessed=4 * array.size, transcendentals=0
            ),
            name="assemble",
        )(places, array, *held)
    return out


def gather(halves, count):
    axes = wide_axes(count)
    orders = ((axes[0], axes[-1]) + tuple(axes[1:-1]), tuple(axes))
    rows = halves[0].shape[0]
    pieces, first = [], 0
    for half, order in zip(halves, orders):
        parts, masks = gather_slots(half, count, order)
        pieces += [(p, m, first) for p, m in zip(parts, masks)]
        first += half.shape[1]
    full = assemble(pieces, count, rows, first)
    return full.reshape(count * rows, first)


def scatter_half(grad, count, order_axes):
    axes = wide_axes(count)
    lengths = [length for _, length in axes]
    rows, cols = grad.shape[1:]
    held = grad.reshape(*lengths, rows, cols)
    me = lax.axis_index("wide")
    left = list(range(len(axes)))
    for axis in order_axes:
        stride, length = axes[axis]
        place = (me // stride) % length
        where = left.index(axis)
        total = lax.dynamic_index_in_dim(held, place, where, keepdims=False).astype(F32)
        for step in range(1, length):
            out = lax.dynamic_index_in_dim(held, place ^ step, where, keepdims=False)
            total = total + push(out.astype(BF16), count, step * stride).astype(F32)
        held = total
        left.remove(axis)
    return held


def scatter(grad, count, split):
    cols = grad.shape[1]
    whole = grad.reshape(count, -1, cols)
    last = len(wide_axes(count)) - 1
    orders = (tuple(range(last, -1, -1)), tuple(range(1, last)) + (last, 0))
    return jnp.concatenate(
        [
            scatter_half(whole[:, :, :split], count, orders[0]),
            scatter_half(whole[:, :, split:], count, orders[1]),
        ],
        axis=1,
    )


def turn(u, cos, sin, low):
    lane = lax.broadcasted_iota(jnp.int32, u.shape, 1)
    quarter = HEAD // 4
    other = jnp.where(
        (lane // quarter) % 2 == 0,
        pltpu.roll(u, PAD - quarter, 1),
        pltpu.roll(u, quarter, 1),
    )
    return (u * cos + other * sin).astype(low)


def forward_attention(qkv, cos, sin, seg_col, seg_row, heads):
    two, batches, half, width = qkv.shape
    count = two * half
    inner = heads * HEAD
    scale = HEAD ** (-0.5)

    def body(qkv_ref, cos_ref, sin_ref, col_ref, row_ref, o_ref, q_ref, k_ref, v_ref, lse_ref):
        cos = cos_ref[...].reshape(count, PAD)
        sin = sin_ref[...].reshape(count, PAD)
        same = col_ref[...].reshape(count, 1) == row_ref[0]
        lane = lax.broadcasted_iota(jnp.int32, (count, PAD), 1)
        sums = jnp.zeros((count, PAD), F32)
        for h in range(heads):
            def part(which):
                start = which * inner + h * HEAD
                return qkv_ref[:, :, :, pl.ds(start, PAD)].reshape(count, PAD)

            q = turn(part(0), cos, sin, BF16)
            k = turn(part(1), cos, sin, BF16)
            v = jnp.where(lane < HEAD, part(2), 0.0).astype(BF16)
            scores = jnp.where(same, dot_nt(q, k) * scale, -1e30)
            top = jnp.max(scores, axis=1, keepdims=True)
            expo = jnp.exp(scores - top)
            total = jnp.sum(expo, axis=1, keepdims=True)
            probs = (expo * (1.0 / total)).astype(BF16)
            o = dot(probs, v).astype(BF16)
            o_ref[:, :, :, pl.ds(h * HEAD, HEAD)] = o[:, :HEAD].reshape(two, 1, half, HEAD)
            q_ref[0, h], k_ref[0, h], v_ref[0, h] = q, k, v
            sums = jnp.where(lane == h, top + jnp.log(total), sums)
        lse_ref[0] = sums

    def four(last):
        return pl.BlockSpec((two, 1, half, last), lambda m: (0, m, 0, 0))

    kept = jax.ShapeDtypeStruct((batches, heads, count, PAD), BF16)
    kept_spec = pl.BlockSpec((1, heads, count, PAD), lambda m: (m, 0, 0, 0))
    return pl.pallas_call(
        body,
        grid=(batches,),
        in_specs=[
            four(width),
            four(PAD),
            four(PAD),
            four(1),
            pl.BlockSpec((1, 1, count), lambda m: (m, 0, 0)),
        ],
        out_specs=[
            four(inner),
            kept_spec,
            kept_spec,
            kept_spec,
            pl.BlockSpec((1, count, PAD), lambda m: (m, 0, 0)),
        ],
        out_shape=[
            jax.ShapeDtypeStruct((two, batches, half, inner), BF16),
            kept,
            kept,
            kept,
            jax.ShapeDtypeStruct((batches, count, PAD), F32),
        ],
        compiler_params=pltpu.CompilerParams(vmem_limit_bytes=VMEM),
        cost_estimate=pl.CostEstimate(
            flops=4 * batches * heads * count * count * PAD,
            bytes_accessed=qkv.size * 4 + 4 * batches * heads * count * PAD * 2,
            transcendentals=batches * heads * count * count,
        ),
        name="attention_fwd",
    )(qkv, cos, sin, seg_col, seg_row)


def backward_attention(d_o, q, k, v, lse, cos, sin, seg_col, seg_row, width):
    two, batches, half, inner = d_o.shape
    heads = q.shape[1]
    count = two * half
    scale = HEAD ** (-0.5)

    def body(do_ref, q_ref, k_ref, v_ref, lse_ref, cos_ref, sin_ref, col_ref, row_ref, out_ref):
        cos = cos_ref[...].reshape(count, PAD)
        sin = -sin_ref[...].reshape(count, PAD)
        same = col_ref[...].reshape(count, 1) == row_ref[0]
        out_ref[...] = jnp.zeros_like(out_ref)
        for h in range(heads):
            q, k, v = q_ref[0, h], k_ref[0, h], v_ref[0, h]
            do = do_ref[:, :, :, pl.ds(h * HEAD, HEAD)].reshape(count, HEAD)
            do = jnp.concatenate([do, jnp.zeros((count, PAD - HEAD), BF16)], axis=1)
            scores = jnp.where(same, dot_nt(q, k) * scale, -1e30)
            probs = jnp.exp(scores - lse_ref[0][:, h : h + 1])
            d_probs = dot_nt(do, v)
            delta = jnp.sum(probs * d_probs, axis=1, keepdims=True)
            d_s = (probs * (d_probs - delta)).astype(BF16)
            d_q = turn(dot(d_s, k) * scale, cos, sin, BF16)
            d_k = turn(dot_tn(d_s, q) * scale, cos, sin, BF16)
            d_v = dot_tn(probs.astype(BF16), do).astype(BF16)
            for which, value in enumerate((d_q, d_k, d_v)):
                out_ref[:, :, :, pl.ds(which * inner + h * HEAD, HEAD)] = value[:, :HEAD].reshape(
                    two, 1, half, HEAD
                )

    def four(last):
        return pl.BlockSpec((two, 1, half, last), lambda m: (0, m, 0, 0))

    kept_spec = pl.BlockSpec((1, heads, count, PAD), lambda m: (m, 0, 0, 0))
    return pl.pallas_call(
        body,
        grid=(batches,),
        in_specs=[
            four(inner),
            kept_spec,
            kept_spec,
            kept_spec,
            pl.BlockSpec((1, count, PAD), lambda m: (m, 0, 0)),
            four(PAD),
            four(PAD),
            four(1),
            pl.BlockSpec((1, 1, count), lambda m: (m, 0, 0)),
        ],
        out_specs=four(width),
        out_shape=jax.ShapeDtypeStruct((two, batches, half, width), BF16),
        compiler_params=pltpu.CompilerParams(vmem_limit_bytes=VMEM),
        cost_estimate=pl.CostEstimate(
            flops=10 * batches * heads * count * count * PAD,
            bytes_accessed=4 * batches * heads * count * PAD * 2 + 2 * batches * count * width,
            transcendentals=batches * heads * count * count,
        ),
        name="attention_bwd",
    )(d_o, q, k, v, lse, cos, sin, seg_col, seg_row)


def layer_stats(values):
    centred = values - jnp.mean(values, axis=-1, keepdims=True)
    inverse = lax.rsqrt(jnp.mean(centred * centred, axis=-1, keepdims=True) + 1e-06)
    return (centred * inverse, inverse)


def layer_back(grad, normed, inverse):
    mean_grad = jnp.mean(grad, axis=-1, keepdims=True)
    mean_mix = jnp.mean(grad * normed, axis=-1, keepdims=True)
    return (grad - mean_grad - normed * mean_mix) * inverse


def turn_tables(rows, cols):
    quarter = HEAD // 4
    freq = 10000.0 ** (-jnp.arange(quarter, dtype=F32) / quarter)
    row = rows.astype(F32)[:, None] * freq
    col = cols.astype(F32)[:, None] * freq
    rest = jnp.zeros((rows.shape[0], PAD - HEAD), F32)
    cos = jnp.concatenate([jnp.cos(row)] * 2 + [jnp.cos(col)] * 2 + [rest], axis=1)
    sin = jnp.concatenate(
        [-jnp.sin(row), jnp.sin(row), -jnp.sin(col), jnp.sin(col), rest], axis=1
    )
    return cos, sin


def by_core(mine, theirs, me, axis):
    first = jnp.where(me == 0, mine, theirs)
    second = jnp.where(me == 0, theirs, mine)
    return jnp.concatenate([first, second], axis=axis)


def shards(
    hidden_in,
    cond_vec,
    seg_ids,
    grid_pos,
    out_grad,
    w_ada,
    b_ada,
    w_qkv,
    b_qkv,
    w_out,
    b_out,
    w_gate,
    w_up,
    w_down,
):
    count = lax.axis_size("wide")
    cores = lax.axis_size("narrow")
    devices = count * cores
    core = lax.axis_index("narrow")
    batches, _, half, width = hidden_in.shape
    slots = cond_vec.shape[2]
    own = batches * half
    heads = HEADS // cores
    inner = heads * HEAD
    rows = w_qkv.shape[0]
    both = ("wide", "narrow")

    by_half = jnp.concatenate(
        [
            w_qkv.reshape(rows, 3, cores, inner).swapaxes(1, 2).reshape(rows, cores, 3 * inner),
            w_out.reshape(rows, cores, width // cores),
        ],
        axis=2,
    )
    mine = lax.dynamic_index_in_dim(by_half, core, 1, keepdims=False)
    theirs = lax.dynamic_index_in_dim(by_half, 1 - core, 1, keepdims=False)
    att = by_core(mine, swap(theirs), core, 0)
    mid = att.shape[1] // 256 * 128
    att = gather((att[:, :mid], att[:, mid:]), count)
    qkv_cols = (3 * inner + 127) // 128 * 128
    qkv_w = att[:, :qkv_cols]
    out_half = att[:, 3 * inner :]
    out_w = by_core(out_half, swap(out_half), core, 1)
    ff = gather((w_gate, w_up), count)
    hidden = w_gate.shape[1]
    gate_w, up_w = ff[:, :hidden], ff[:, hidden:]
    down_t = w_down.T
    cut = hidden // 256 * 128
    down_w = gather((down_t[:, :cut], down_t[:, cut:]), count)

    biases = lax.all_gather(jnp.concatenate([b_qkv, b_out]), both, axis=0)
    n_b = b_qkv.shape[0]
    qkv_b = biases[:, :n_b].reshape(3, cores, inner).astype(F32)
    qkv_b = lax.dynamic_index_in_dim(qkv_b, core, 1, keepdims=False).reshape(-1)
    qkv_b = jnp.pad(qkv_b, (0, qkv_cols - 3 * inner))
    out_b = biases[:, n_b:].reshape(-1).astype(F32)

    ada_cols = w_ada.shape[1] // devices
    ada = lax.all_to_all(
        w_ada.reshape(rows, devices, ada_cols).swapaxes(0, 1), both, 0, 0
    ).reshape(devices * rows, ada_cols)
    cond = jax.nn.silu(cond_vec[:, 0].astype(F32)).astype(BF16).reshape(batches * slots, width)
    cond_all = lax.all_gather(cond, "wide", axis=0)
    modul = dot(cond_all.reshape(-1, width), ada) + b_ada.astype(F32)
    modul = modul.reshape(count, 1, batches * slots, ada_cols)
    modul = jnp.broadcast_to(modul, (count, cores, batches * slots, ada_cols))
    modul = lax.all_to_all(
        modul.reshape(devices, batches * slots, ada_cols), both, 0, 0
    )
    modul = modul.swapaxes(0, 1).reshape(batches * slots, 6 * width)

    segs = seg_ids[:, 0].reshape(batches, cores, half)
    seg_own = lax.dynamic_index_in_dim(segs, core, 1, keepdims=False)
    seg_other = lax.dynamic_index_in_dim(segs, 1 - core, 1, keepdims=False)
    seg_two = jnp.stack([seg_own, seg_other])
    seg_col = seg_two[..., None]
    seg_row = seg_two.swapaxes(0, 1).reshape(batches, 1, cores * half)
    slot_ids = seg_own + slots * jnp.arange(batches)[:, None]
    picker = (slot_ids.reshape(own, 1) == jnp.arange(batches * slots)[None]).astype(F32)
    places = jnp.stack([grid_pos[0, :, 0], grid_pos[1, :, 0]]).reshape(2, own)
    places = jnp.stack([places, swap(places)], axis=1).reshape(2, 2 * own)
    cos, sin = turn_tables(places[0], places[1])
    cos = cos.reshape(2, batches, half, PAD)
    sin = sin.reshape(2, batches, half, PAD)

    def with_other(x):
        return jnp.concatenate([x, swap(x)], axis=0)

    per_tok = jnp.dot(picker, modul, precision=HIGHEST)
    shift1, scale1, gate1, shift2, scale2, gate2 = jnp.split(per_tok, 6, axis=1)
    inputs = hidden_in.reshape(own, width).astype(F32)
    normed1, inverse1 = layer_stats(inputs)
    a_low = with_other((normed1 * (1.0 + scale1) + shift1).astype(BF16))
    qkv = dot(a_low, qkv_w) + qkv_b
    o_heads, q, k, v, lse = forward_attention(
        qkv.reshape(2, batches, half, qkv_cols), cos, sin, seg_col, seg_row, heads
    )
    o_heads = o_heads.reshape(2, own, inner)
    o_low = by_core(o_heads[0], swap(o_heads[1]), core, 1)
    branch = dot(o_low, out_w) + out_b
    mixed = inputs + gate1 * branch
    normed2, inverse2 = layer_stats(mixed)
    c_low = with_other((normed2 * (1.0 + scale2) + shift2).astype(BF16))
    d_out = out_grad.reshape(own, width).astype(F32)
    d_mlp_low = with_other((d_out * gate2).astype(BF16))

    gate = dot(c_low, gate_w)
    up = dot(c_low, up_w)
    sigma = jax.nn.sigmoid(gate)
    active = gate * sigma
    hid_low = (active * up).astype(BF16)
    g_down = dot_tn(d_mlp_low, hid_low).astype(BF16)
    d_hid = dot(d_mlp_low, down_w)
    d_gate_low = (d_hid * up * sigma * (1.0 + gate * (1.0 - sigma))).astype(BF16)
    d_up_low = (d_hid * active).astype(BF16)
    g_gate = dot_tn(c_low, d_gate_low).astype(BF16)
    g_up = dot_tn(c_low, d_up_low).astype(BF16)
    s_down = scatter(g_down, count, cut)
    s_gate_up = scatter(jnp.concatenate([g_gate, g_up], axis=1), count, hidden)

    def sum_cores(part):
        return part[:own] + swap(part[own:].astype(BF16)).astype(F32)

    d_c = sum_cores(dot_nt(d_gate_low, gate_w) + dot_nt(d_up_low, up_w))
    mlp = sum_cores(dot_nt(hid_low, down_w))
    result = mixed + gate2 * mlp
    d_gate2 = d_out * mlp
    d_scale2 = d_c * normed2
    d_mixed = d_out + layer_back(d_c * (1.0 + scale2), normed2, inverse2)
    d_gate1 = d_mixed * branch
    d_branch_low = (d_mixed * gate1).astype(BF16)
    g_out_b = jnp.sum(d_branch_low.astype(F32), axis=0)
    d_o = dot_nt(d_branch_low, out_w).astype(BF16).reshape(own, cores, inner)
    d_o_mine = lax.dynamic_index_in_dim(d_o, core, 1, keepdims=False)
    d_o_theirs = lax.dynamic_index_in_dim(d_o, 1 - core, 1, keepdims=False)
    d_o_heads = jnp.stack([d_o_mine, swap(d_o_theirs)]).reshape(2, batches, half, inner)
    g_out = dot_tn(o_low, d_branch_low).reshape(width, cores, width // cores)
    g_out_mine = lax.dynamic_index_in_dim(g_out, core, 1, keepdims=False)
    g_out_theirs = lax.dynamic_index_in_dim(g_out, 1 - core, 1, keepdims=False)
    g_out = (g_out_mine + swap(g_out_theirs.astype(BF16)).astype(F32)).astype(BF16)
    s_out = scatter(g_out, count, width // cores // 256 * 128)

    d_qkv = backward_attention(
        d_o_heads, q, k, v, lse, cos, sin, seg_col, seg_row, qkv_cols
    ).reshape(2 * own, qkv_cols)
    g_qkv = dot_tn(a_low, d_qkv).astype(BF16)
    s_qkv = scatter(g_qkv, count, qkv_cols // 256 * 128)[:, : 3 * inner]
    g_qkv_b = jnp.sum(d_qkv.astype(F32), axis=0)[: 3 * inner]
    d_a = sum_cores(dot_nt(d_qkv, qkv_w))
    d_scale1 = d_a * normed1
    d_input = d_mixed + layer_back(d_a * (1.0 + scale1), normed1, inverse1)

    d_modul = jnp.concatenate(
        [
            lax.dot_general(picker, d, (((0,), (0,)), ((), ())), precision=HIGHEST)
            for d in (d_a, d_scale1, d_gate1, d_c, d_scale2, d_gate2)
        ],
        axis=1,
    )
    d_modul = d_modul.reshape(batches * slots, devices, ada_cols).swapaxes(0, 1)
    b_parts = jnp.zeros((3, cores, inner), F32)
    b_parts = lax.dynamic_update_index_in_dim(b_parts, g_qkv_b.reshape(3, 1, inner), core, 1)
    bias_part = jnp.concatenate(
        [b_parts.reshape(devices, -1), g_out_b.reshape(devices, -1)], axis=1
    )
    n_bias = bias_part.shape[1]
    bias_rows = -(-n_bias // ada_cols)
    bias_part = jnp.pad(bias_part, ((0, 0), (0, bias_rows * ada_cols - n_bias)))
    message = jnp.concatenate(
        [d_modul, bias_part.reshape(devices, bias_rows, ada_cols)], axis=1
    )
    message = lax.all_to_all(message, both, 0, 0)
    g_bias = jnp.sum(message[:, batches * slots :], axis=0).reshape(-1)
    g_qkv_b, g_out_b = g_bias[:n_b], g_bias[n_b:n_bias]
    d_modul = jnp.sum(
        message[:, : batches * slots].reshape(count, cores, batches * slots, ada_cols), axis=1
    ).reshape(-1, ada_cols)
    g_ada_b = jnp.sum(d_modul, axis=0)
    g_ada = lax.dot_general(
        cond_all.reshape(-1, width).astype(F32),
        d_modul,
        (((0,), (0,)), ((), ())),
        precision=HIGHEST,
    )
    g_ada = lax.all_to_all(g_ada.reshape(devices, rows, ada_cols), both, 0, 0)
    g_ada = g_ada.swapaxes(0, 1).reshape(rows, 6 * width)

    s_att = jnp.concatenate([s_qkv, s_out], axis=1).reshape(cores, rows, -1)
    s_mine = lax.dynamic_index_in_dim(s_att, core, 0, keepdims=False)
    s_theirs = swap(lax.dynamic_index_in_dim(s_att, 1 - core, 0, keepdims=False))
    s_first = jnp.where(core == 0, s_mine, s_theirs)
    s_second = jnp.where(core == 0, s_theirs, s_mine)
    s_both = jnp.stack([s_first, s_second], axis=1)
    g_qkv = (
        s_both[:, :, : 3 * inner].reshape(rows, cores, 3, inner).swapaxes(1, 2).reshape(rows, -1)
    )
    g_out = s_both[:, :, 3 * inner :].reshape(rows, width)

    def tokens(x):
        return x.reshape(batches, 1, half, width)

    return (
        tokens(result),
        tokens(d_input),
        g_ada,
        g_ada_b,
        g_qkv,
        g_qkv_b,
        g_out,
        g_out_b,
        s_gate_up[:, :hidden],
        s_gate_up[:, hidden:],
        s_down.T,
    )


def solution(mesh):
    both = ("wide", "narrow")
    in_specs = (
        P(None, "wide", "narrow", None),
        P(None, "wide", None, None),
        P(None, "wide", None),
        P(None, None, "wide", "narrow"),
        P(None, "wide", "narrow", None),
        P(both, None),
        P(both),
        P(both, None),
        P(both),
        P(both, None),
        P(both),
        P("wide", "narrow"),
        P("wide", "narrow"),
        P("narrow", "wide"),
    )
    out_specs = (
        P(None, "wide", "narrow", None),
        P(None, "wide", "narrow", None),
        P(both, None),
        P(both),
        P(both, None),
        P(both),
        P(both, None),
        P(both),
        P("wide", "narrow"),
        P("wide", "narrow"),
        P("narrow", "wide"),
    )
    return jax.shard_map(shards, mesh=mesh, in_specs=in_specs, out_specs=out_specs, check_vma=False)
```

```python
import functools

import jax
import jax.numpy as jnp
from jax import lax
from jax.experimental import pallas as pl
from jax.experimental.pallas import tpu as pltpu
from jax.sharding import PartitionSpec as P

HEADS = 16
HEAD = 72
PAD = 128
F32 = jnp.float32
BF16 = jnp.bfloat16
HIGHEST = lax.Precision.HIGHEST
VMEM = 56 * 2**20


def dot(a, b):
    return jnp.dot(a, b, preferred_element_type=F32)


def dot_nt(a, b):
    return lax.dot_general(a, b, (((1,), (1,)), ((), ())), preferred_element_type=F32)


def dot_tn(a, b):
    return lax.dot_general(a, b, (((0,), (0,)), ((), ())), preferred_element_type=F32)


def wide_axes(count):
    if count == 16:
        lengths = (4, 2, 2)
    elif count == 64:
        lengths = (4, 4, 4)
    else:
        lengths = (2,) * (count.bit_length() - 1)
    axes, stride = [], count
    for length in lengths:
        stride //= length
        axes.append((stride, length))
    return axes


def push(x, count, mask):
    return lax.ppermute(x, "wide", [(i, i ^ mask) for i in range(count)])


def swap(x):
    return lax.ppermute(x, "narrow", [(0, 1), (1, 0)])


def gather_slots(own, count, order):
    parts, masks = [own[None]], [[0]]
    for stride, length in order:
        have = parts[0] if len(parts) == 1 else jnp.concatenate(parts, axis=0)
        seen = sum(masks, [])
        parts, masks = [have], [seen]
        for step in range(1, length):
            parts.append(push(have, count, step * stride))
            masks.append([m ^ (step * stride) for m in seen])
    return parts, masks


def assemble(pieces, count, rows, cols):
    out = None
    me = lax.axis_index("wide")
    for array, masks, first in pieces:
        width = array.shape[2]
        places = me ^ jnp.array(masks, jnp.int32)

        def body(place_ref, in_ref, *refs):
            refs[-1][...] = in_ref[...]

        held = [] if out is None else [out]
        out = pl.pallas_call(
            body,
            out_shape=jax.ShapeDtypeStruct((count, rows, cols), BF16),
            grid_spec=pltpu.PrefetchScalarGridSpec(
                num_scalar_prefetch=1,
                grid=(len(masks),),
                in_specs=[pl.BlockSpec((1, rows, width), lambda s, p: (s, 0, 0))]
                + [pl.BlockSpec(memory_space=pl.ANY)] * len(held),
                out_specs=pl.BlockSpec((1, rows, width), lambda s, p, c=first // width: (p[s], 0, c)),
            ),
            input_output_aliases={2: 0} if held else {},
            cost_estimate=pl.CostEstimate(
                flops=0, bytes_accessed=4 * array.size, transcendentals=0
            ),
            name="assemble",
        )(places, array, *held)
    return out


def gather(halves, count):
    axes = wide_axes(count)
    orders = ((axes[0], axes[-1]) + tuple(axes[1:-1]), tuple(axes))
    rows = halves[0].shape[0]
    pieces, first = [], 0
    for half, order in zip(halves, orders):
        parts, masks = gather_slots(half, count, order)
        pieces += [(p, m, first) for p, m in zip(parts, masks)]
        first += half.shape[1]
    full = assemble(pieces, count, rows, first)
    return full.reshape(count * rows, first)


def scatter_half(grad, count, order_axes):
    axes = wide_axes(count)
    lengths = [length for _, length in axes]
    rows, cols = grad.shape[1:]
    held = grad.reshape(*lengths, rows, cols)
    me = lax.axis_index("wide")
    left = list(range(len(axes)))
    for axis in order_axes:
        stride, length = axes[axis]
        place = (me // stride) % length
        where = left.index(axis)
        total = lax.dynamic_index_in_dim(held, place, where, keepdims=False).astype(F32)
        for step in range(1, length):
            out = lax.dynamic_index_in_dim(held, place ^ step, where, keepdims=False)
            total = total + push(out.astype(BF16), count, step * stride).astype(F32)
        held = total
        left.remove(axis)
    return held


def scatter(grad, count, split):
    cols = grad.shape[1]
    whole = grad.reshape(count, -1, cols)
    last = len(wide_axes(count)) - 1
    orders = (tuple(range(last, -1, -1)), tuple(range(1, last)) + (last, 0))
    return jnp.concatenate(
        [
            scatter_half(whole[:, :, :split], count, orders[0]),
            scatter_half(whole[:, :, split:], count, orders[1]),
        ],
        axis=1,
    )


def turn(u, cos, sin, low):
    lane = lax.broadcasted_iota(jnp.int32, u.shape, 1)
    quarter = HEAD // 4
    other = jnp.where(
        (lane // quarter) % 2 == 0,
        pltpu.roll(u, PAD - quarter, 1),
        pltpu.roll(u, quarter, 1),
    )
    return (u * cos + other * sin).astype(low)


def forward_attention(qkv, cos, sin, seg_col, seg_row, heads):
    two, batches, half, width = qkv.shape
    count = two * half
    inner = heads * HEAD
    scale = HEAD ** (-0.5)

    def body(qkv_ref, cos_ref, sin_ref, col_ref, row_ref, o_ref, q_ref, k_ref, v_ref, lse_ref):
        cos = cos_ref[...].reshape(count, PAD)
        sin = sin_ref[...].reshape(count, PAD)
        same = col_ref[...].reshape(count, 1) == row_ref[0]
        lane = lax.broadcasted_iota(jnp.int32, (count, PAD), 1)
        sums = jnp.zeros((count, PAD), F32)
        for h in range(heads):
            def part(which):
                start = which * inner + h * HEAD
                return qkv_ref[:, :, :, pl.ds(start, PAD)].reshape(count, PAD)

            q = turn(part(0), cos, sin, BF16)
            k = turn(part(1), cos, sin, BF16)
            v = jnp.where(lane < HEAD, part(2), 0.0).astype(BF16)
            scores = jnp.where(same, dot_nt(q, k) * scale, -1e30)
            top = jnp.max(scores, axis=1, keepdims=True)
            expo = jnp.exp(scores - top)
            total = jnp.sum(expo, axis=1, keepdims=True)
            probs = (expo * (1.0 / total)).astype(BF16)
            o = dot(probs, v).astype(BF16)
            o_ref[:, :, :, pl.ds(h * HEAD, HEAD)] = o[:, :HEAD].reshape(two, 1, half, HEAD)
            q_ref[0, h], k_ref[0, h], v_ref[0, h] = q, k, v
            sums = jnp.where(lane == h, top + jnp.log(total), sums)
        lse_ref[0] = sums

    def four(last):
        return pl.BlockSpec((two, 1, half, last), lambda m: (0, m, 0, 0))

    kept = jax.ShapeDtypeStruct((batches, heads, count, PAD), BF16)
    kept_spec = pl.BlockSpec((1, heads, count, PAD), lambda m: (m, 0, 0, 0))
    return pl.pallas_call(
        body,
        grid=(batches,),
        in_specs=[
            four(width),
            four(PAD),
            four(PAD),
            four(1),
            pl.BlockSpec((1, 1, count), lambda m: (m, 0, 0)),
        ],
        out_specs=[
            four(inner),
            kept_spec,
            kept_spec,
            kept_spec,
            pl.BlockSpec((1, count, PAD), lambda m: (m, 0, 0)),
        ],
        out_shape=[
            jax.ShapeDtypeStruct((two, batches, half, inner), BF16),
            kept,
            kept,
            kept,
            jax.ShapeDtypeStruct((batches, count, PAD), F32),
        ],
        compiler_params=pltpu.CompilerParams(vmem_limit_bytes=VMEM),
        cost_estimate=pl.CostEstimate(
            flops=4 * batches * heads * count * count * PAD,
            bytes_accessed=qkv.size * 4 + 4 * batches * heads * count * PAD * 2,
            transcendentals=batches * heads * count * count,
        ),
        name="attention_fwd",
    )(qkv, cos, sin, seg_col, seg_row)


def backward_attention(d_o, q, k, v, lse, cos, sin, seg_col, seg_row, width):
    two, batches, half, inner = d_o.shape
    heads = q.shape[1]
    count = two * half
    scale = HEAD ** (-0.5)

    def body(do_ref, q_ref, k_ref, v_ref, lse_ref, cos_ref, sin_ref, col_ref, row_ref, out_ref):
        cos = cos_ref[...].reshape(count, PAD)
        sin = -sin_ref[...].reshape(count, PAD)
        same = col_ref[...].reshape(count, 1) == row_ref[0]
        out_ref[...] = jnp.zeros_like(out_ref)
        for h in range(heads):
            q, k, v = q_ref[0, h], k_ref[0, h], v_ref[0, h]
            do = do_ref[:, :, :, pl.ds(h * HEAD, HEAD)].reshape(count, HEAD)
            do = jnp.concatenate([do, jnp.zeros((count, PAD - HEAD), BF16)], axis=1)
            scores = jnp.where(same, dot_nt(q, k) * scale, -1e30)
            probs = jnp.exp(scores - lse_ref[0][:, h : h + 1])
            d_probs = dot_nt(do, v)
            delta = jnp.sum(probs * d_probs, axis=1, keepdims=True)
            d_s = (probs * (d_probs - delta)).astype(BF16)
            d_q = turn(dot(d_s, k) * scale, cos, sin, BF16)
            d_k = turn(dot_tn(d_s, q) * scale, cos, sin, BF16)
            d_v = dot_tn(probs.astype(BF16), do).astype(BF16)
            for which, value in enumerate((d_q, d_k, d_v)):
                out_ref[:, :, :, pl.ds(which * inner + h * HEAD, HEAD)] = value[:, :HEAD].reshape(
                    two, 1, half, HEAD
                )

    def four(last):
        return pl.BlockSpec((two, 1, half, last), lambda m: (0, m, 0, 0))

    kept_spec = pl.BlockSpec((1, heads, count, PAD), lambda m: (m, 0, 0, 0))
    return pl.pallas_call(
        body,
        grid=(batches,),
        in_specs=[
            four(inner),
            kept_spec,
            kept_spec,
            kept_spec,
            pl.BlockSpec((1, count, PAD), lambda m: (m, 0, 0)),
            four(PAD),
            four(PAD),
            four(1),
            pl.BlockSpec((1, 1, count), lambda m: (m, 0, 0)),
        ],
        out_specs=four(width),
        out_shape=jax.ShapeDtypeStruct((two, batches, half, width), BF16),
        compiler_params=pltpu.CompilerParams(vmem_limit_bytes=VMEM),
        cost_estimate=pl.CostEstimate(
            flops=10 * batches * heads * count * count * PAD,
            bytes_accessed=4 * batches * heads * count * PAD * 2 + 2 * batches * count * width,
            transcendentals=batches * heads * count * count,
        ),
        name="attention_bwd",
    )(d_o, q, k, v, lse, cos, sin, seg_col, seg_row)


ZS, YS, XS = 4, 2, 2
MESH = pl.DeviceIdType.MESH


def place(wide):
    return wide // (YS * XS), (wide // XS) % YS, wide % XS


def wide_of(z, y, x):
    return (z * YS + y) * XS + x


class Gather:
    def __init__(self, own, full, first, width, order, send, recv, base, here, core):
        z, y, x = here
        cols = pl.ds(first, width)

        def remote(src, dst, sem, wide):
            return pltpu.make_async_remote_copy(
                src_ref=src,
                dst_ref=dst,
                send_sem=send.at[base + sem],
                recv_sem=recv.at[base + sem],
                device_id=(wide, core),
                device_id_type=MESH,
            )

        self.line = [
            remote(
                own.at[:, cols],
                full.at[z, y, x, :, cols],
                step - 1,
                wide_of((z + step) % ZS, y, x),
            )
            for step in range(1, ZS)
        ]
        over_x, over_y = wide_of(z, y, 1 - x), wide_of(z, 1 - y, x)
        one = full.at[:, y, x, :, cols]
        if order == "xy":
            two = full.at[:, y, :, :, cols]
            self.second = [remote(one, one, ZS - 1, over_x)]
            self.third = [remote(two, two, ZS, over_y)]
        else:
            two = full.at[:, :, x, :, cols]
            self.second = [remote(one, one, ZS - 1, over_y)]
            self.third = [remote(two, two, ZS, over_x)]


GATHER_SEMS = ZS + 1


def start(copies):
    for c in copies:
        c.start()


def arrive(copies):
    for c in copies:
        c.wait_recv()


def leave(copies):
    for c in copies:
        c.wait_send()


def stats(values):
    centred = values - jnp.mean(values, axis=-1, keepdims=True)
    inverse = lax.rsqrt(jnp.mean(centred * centred, axis=-1, keepdims=True) + 1e-06)
    return centred * inverse, inverse


def forward_body(
    sizes,
    x_ref, dy_ref, modul_ref, slot_ref, col_ref, row_ref, cos_ref, sin_ref,
    qkvb_ref, outb_ref, att_own, gate_own, up_own, down_own,
    att_out, wout_out, gate_all, up_all, down_all, a_out, dm_out, q_out, k_out, v_out,
    lse_out, o_out, oth_out, branch_out, mixed_out, c_out,
    att, wqkv, wo_mine, wo_other, wout, a_all, dm_all, qkv, q_s, k_s, v_s, lse_s,
    o_mine, o_other, branch, mixed, c_all, hi_ref, lo_ref, send, recv, local,
):
    batches, half, width, heads, slots = sizes
    own = batches * half
    inner = heads * HEAD
    count = 2 * half
    qkv_cols = wqkv.shape[1]
    out_cols = wo_mine.shape[1]
    wide, core = lax.axis_index("wide"), lax.axis_index("narrow")
    here = place(wide)
    z, y, x = here
    scale = HEAD ** (-0.5)
    sem = [0]
    saves = []

    def local_sem():
        sem[0] += 1
        return local.at[sem[0] - 1]

    def save(src, dst):
        c = pltpu.make_async_copy(src, dst, local_sem())
        c.start()
        saves.append(c)

    remote_sem = [0]

    def group(own_ref, full, first, width_, cut):
        parts = []
        for a, b, order in ((0, cut, "xy"), (cut, width_, "yx")):
            parts.append(
                Gather(own_ref, full, first + a, b - a, order, send, recv, remote_sem[0], here, core)
            )
            remote_sem[0] += GATHER_SEMS
        mine = pltpu.make_async_copy(
            own_ref.at[:, pl.ds(first, width_)],
            full.at[z, y, x, :, pl.ds(first, width_)],
            local_sem(),
        )
        mine.start()
        return [sum((getattr(p, k) for p in parts), []) for k in ("line", "second", "third")], mine

    def exchange(src, dst):
        c = pltpu.make_async_remote_copy(
            src_ref=src,
            dst_ref=dst,
            send_sem=send.at[remote_sem[0]],
            recv_sem=recv.at[remote_sem[0]],
            device_id=(wide, 1 - core),
            device_id_type=MESH,
        )
        remote_sem[0] += 1
        c.start()
        return c

    barrier = pltpu.get_barrier_semaphore()
    peers = [(wide_of((z + s) % ZS, y, x), core) for s in range(1, ZS)]
    peers += [(wide_of(z, y, 1 - x), core), (wide_of(z, 1 - y, x), core), (wide, 1 - core)]
    for peer in peers:
        pl.semaphore_signal(barrier, inc=1, device_id=peer, device_id_type=MESH)
    pl.semaphore_wait(barrier, len(peers))

    (out1, out2, out3), out_mine = group(att_own, att, qkv_cols, out_cols, out_cols // 256 * 128)
    (qkv1, qkv2, qkv3), qkv_mine = group(att_own, att, 0, qkv_cols, qkv_cols // 256 * 128)
    hidden = gate_own.shape[1]
    (gate1, gate2, gate3), gate_mine = group(gate_own, gate_all, 0, hidden, hidden // 2)
    (up1, up2, up3), up_mine = group(up_own, up_all, 0, hidden, hidden // 2)
    (down1, down2, down3), down_mine = group(down_own, down_all, 0, hidden, hidden // 2)

    start(out1)
    tile = 128
    high = modul_ref[...].astype(BF16)
    hi_ref[...] = high
    lo_ref[...] = (modul_ref[...] - high.astype(F32)).astype(BF16)

    def modul(onehot, part):
        cols = pl.ds(part * width, width)
        return dot(onehot, hi_ref[:, cols]) + dot(onehot, lo_ref[:, cols])

    def onehot_of(rows):
        n = slot_ref[rows, :].shape[0]
        lane = lax.broadcasted_iota(jnp.int32, (n, hi_ref.shape[0]), 1)
        return (slot_ref[rows, :] == lane).astype(F32).astype(BF16)

    @pl.loop(0, own // tile)
    def _(i):
        rows = pl.ds(pl.multiple_of(i * tile, tile), tile)
        onehot = onehot_of(rows)
        normed, _ = stats(x_ref[rows, :].astype(F32))
        a_all[rows, :] = (normed * (1.0 + modul(onehot, 1)) + modul(onehot, 0)).astype(BF16)
        dm_all[rows, :] = (dy_ref[rows, :].astype(F32) * modul(onehot, 5)).astype(BF16)

    a_swap = exchange(a_all.at[pl.ds(0, own)], a_all.at[pl.ds(own, own)])
    dm_swap = exchange(dm_all.at[pl.ds(0, own)], dm_all.at[pl.ds(own, own)])

    arrive(out1)
    start(qkv1)
    out_mine.wait()
    start(out2)
    arrive(out2)
    start(out3)
    arrive(qkv1)
    start(gate1)
    qkv_mine.wait()
    start(qkv2)
    arrive(out3)

    @pl.loop(0, ZS * YS)
    def _(j):
        rows = pl.ds(pl.multiple_of(j * 2 * HEAD, 2 * HEAD), 2 * HEAD)
        pair = [att[j // YS, j % YS, i, :, pl.ds(qkv_cols, out_cols)].astype(F32) for i in range(2)]
        wo_mine[rows, :] = jnp.concatenate(pair, axis=0).astype(BF16)

    wo_swap = exchange(wo_mine, wo_other)
    arrive(qkv2)
    start(qkv3)
    arrive(gate1)
    start(up1)
    gate_mine.wait()
    start(gate2)
    wo_swap.wait_recv()
    first_cols = pl.ds(0, out_cols)
    rest = width - out_cols
    skip = out_cols - rest

    @pl.loop(0, ZS * YS)
    def _(j):
        rows = pl.ds(pl.multiple_of(j * 2 * HEAD, 2 * HEAD), 2 * HEAD)
        mine, other = wo_mine[rows, :], wo_other[rows, :]
        wout[rows, first_cols] = jnp.where(core == 0, mine, other)
        wout[rows, pl.ds(out_cols, rest)] = jnp.where(core == 0, other, mine)[:, skip:]

    save(wout, wout_out)
    a_swap.wait_recv()
    dm_swap.wait_recv()
    save(a_all, a_out)
    save(dm_all, dm_out)
    arrive(qkv3)

    @pl.loop(0, ZS * YS)
    def _(j):
        rows = pl.ds(pl.multiple_of(j * 2 * HEAD, 2 * HEAD), 2 * HEAD)
        pair = [att[j // YS, j % YS, i, :, pl.ds(0, qkv_cols)].astype(F32) for i in range(2)]
        wqkv[rows, :] = jnp.concatenate(pair, axis=0).astype(BF16)

    save(att, att_out)

    @pl.loop(0, 2 * own // 256)
    def _(i):
        rows = pl.ds(pl.multiple_of(i * 256, 256), 256)
        qkv[rows, :] = dot(a_all[rows, :], wqkv[...]) + qkvb_ref[...]

    arrive(gate2)
    start(gate3)
    arrive(up1)
    start(down1)
    up_mine.wait()
    start(up2)

    def both_halves(ref, m, lanes):
        first = ref[pl.ds(pl.multiple_of(m * half, half), half), lanes]
        second = ref[pl.ds(pl.multiple_of(own + m * half, half), half), lanes]
        return jnp.concatenate([first, second], axis=0)

    @pl.loop(0, batches)
    def _(m):
        cos = both_halves(cos_ref, m, slice(None))
        sin = both_halves(sin_ref, m, slice(None))
        same = both_halves(col_ref, m, slice(None)) == row_ref[m]
        lane = lax.broadcasted_iota(jnp.int32, (count, PAD), 1)
        sums = jnp.zeros((count, PAD), F32)
        for h in range(heads):
            def part(which):
                return both_halves(qkv, m, pl.ds(which * inner + h * HEAD, PAD))

            q = turn(part(0), cos, sin, BF16)
            k = turn(part(1), cos, sin, BF16)
            v = jnp.where(lane < HEAD, part(2), 0.0).astype(BF16)
            scores = jnp.where(same, dot_nt(q, k) * scale, -1e30)
            top = jnp.max(scores, axis=1, keepdims=True)
            expo = jnp.exp(scores - top)
            total = jnp.sum(expo, axis=1, keepdims=True)
            probs = (expo * (1.0 / total)).astype(BF16)
            o = dot(probs, v).astype(BF16)[:, :HEAD]
            lanes = pl.ds(h * HEAD, HEAD)
            o_mine[pl.ds(pl.multiple_of(m * half, half), half), lanes] = o[:half]
            o_mine[pl.ds(pl.multiple_of(own + m * half, half), half), lanes] = o[half:]
            q_s[m, h], k_s[m, h], v_s[m, h] = q, k, v
            sums = jnp.where(lane == h, top + jnp.log(total), sums)
            if h == heads // 2:

                @pl.when(m == 0)
                def _():
                    arrive(up2)
                    start(up3)
                    arrive(down1)
                    down_mine.wait()
                    start(down2)

                @pl.when(m == 1)
                def _():
                    arrive(down2)
                    start(down3)

        lse_s[m] = sums

    o_swap = exchange(o_mine.at[pl.ds(own, own)], o_other)
    save(q_s, q_out)
    save(k_s, k_out)
    save(v_s, v_out)
    save(lse_s, lse_out)
    save(o_mine, o_out)
    o_swap.wait_recv()
    save(o_other, oth_out)
    mine_rows = pl.ds(pl.multiple_of(core * inner, 16), inner)
    other_rows = pl.ds(pl.multiple_of((1 - core) * inner, 16), inner)

    @pl.loop(0, own // tile)
    def _(i):
        rows = pl.ds(pl.multiple_of(i * tile, tile), tile)
        out = dot(o_mine[rows, :], wout[mine_rows, :]) + dot(o_other[rows, :], wout[other_rows, :])
        out = out + outb_ref[...]
        onehot = onehot_of(rows)
        branch[rows, :] = out
        mix = x_ref[rows, :].astype(F32) + modul(onehot, 2) * out
        mixed[rows, :] = mix
        normed, _ = stats(mix)
        c_all[rows, :] = (normed * (1.0 + modul(onehot, 4)) + modul(onehot, 3)).astype(BF16)

    c_swap = exchange(c_all.at[pl.ds(0, own)], c_all.at[pl.ds(own, own)])
    save(branch, branch_out)
    save(mixed, mixed_out)
    c_swap.wait_recv()
    save(c_all, c_out)
    arrive(gate3)
    arrive(up3)
    arrive(down3)
    for copies in (out1, out2, out3, qkv1, qkv2, qkv3, gate1, gate2, gate3):
        leave(copies)
    for copies in (up1, up2, up3, down1, down2, down3):
        leave(copies)
    leave([a_swap, dm_swap, wo_swap, o_swap, c_swap])
    for c in saves:
        c.wait()


def forward_call(x, dy, modul, slot, col, row, cos, sin, qkvb, outb, att, gate, up, down, heads):
    own, width = x.shape
    batches = row.shape[0]
    half = own // batches
    inner = heads * HEAD
    rows = att.shape[0]
    qkv_cols = qkvb.shape[1]
    out_cols = att.shape[1] - qkv_cols
    hidden = gate.shape[1]
    slots = (ZS, YS, XS, rows)
    s = jax.ShapeDtypeStruct
    kept = (batches, heads, 2 * half, PAD)
    outs = [
        s(slots + (att.shape[1],), BF16),
        s((width, width), BF16),
        s(slots + (hidden,), BF16),
        s(slots + (hidden,), BF16),
        s(slots + (hidden,), BF16),
        s((2 * own, width), BF16),
        s((2 * own, width), BF16),
        s(kept, BF16),
        s(kept, BF16),
        s(kept, BF16),
        s((batches, 2 * half, PAD), F32),
        s((2 * own, inner), BF16),
        s((own, inner), BF16),
        s((own, width), F32),
        s((own, width), F32),
        s((2 * own, width), BF16),
    ]
    remotes = 10 * GATHER_SEMS + 8
    scratch = [
        pltpu.VMEM(slots + (att.shape[1],), BF16),
        pltpu.VMEM((width, qkv_cols), BF16),
        pltpu.VMEM((width, out_cols), BF16),
        pltpu.VMEM((width, out_cols), BF16),
        pltpu.VMEM((width, width), BF16),
        pltpu.VMEM((2 * own, width), BF16),
        pltpu.VMEM((2 * own, width), BF16),
        pltpu.VMEM((2 * own, qkv_cols), F32),
        pltpu.VMEM(kept, BF16),
        pltpu.VMEM(kept, BF16),
        pltpu.VMEM(kept, BF16),
        pltpu.VMEM((batches, 2 * half, PAD), F32),
        pltpu.VMEM((2 * own, inner), BF16),
        pltpu.VMEM((own, inner), BF16),
        pltpu.VMEM((own, width), F32),
        pltpu.VMEM((own, width), F32),
        pltpu.VMEM((2 * own, width), BF16),
        pltpu.VMEM(modul.shape, BF16),
        pltpu.VMEM(modul.shape, BF16),
        pltpu.SemaphoreType.DMA((remotes,)),
        pltpu.SemaphoreType.DMA((remotes,)),
        pltpu.SemaphoreType.DMA((24,)),
    ]
    sizes = (batches, half, width, heads, modul.shape[0])
    return pl.pallas_call(
        functools.partial(forward_body, sizes),
        out_shape=outs,
        in_specs=[pl.BlockSpec(memory_space=pltpu.VMEM)] * 14,
        out_specs=[pl.BlockSpec(memory_space=pl.ANY)] * len(outs),
        scratch_shapes=scratch,
        compiler_params=pltpu.CompilerParams(
            collective_id=0, has_side_effects=True, vmem_limit_bytes=60 * 2**20
        ),
        name="forward",
    )(x, dy, modul, slot, col, row, cos, sin, qkvb, outb, att, gate, up, down)


def layer_stats(values):
    centred = values - jnp.mean(values, axis=-1, keepdims=True)
    inverse = lax.rsqrt(jnp.mean(centred * centred, axis=-1, keepdims=True) + 1e-06)
    return (centred * inverse, inverse)


def layer_back(grad, normed, inverse):
    mean_grad = jnp.mean(grad, axis=-1, keepdims=True)
    mean_mix = jnp.mean(grad * normed, axis=-1, keepdims=True)
    return (grad - mean_grad - normed * mean_mix) * inverse


def turn_tables(rows, cols):
    quarter = HEAD // 4
    freq = 10000.0 ** (-jnp.arange(quarter, dtype=F32) / quarter)
    row = rows.astype(F32)[:, None] * freq
    col = cols.astype(F32)[:, None] * freq
    rest = jnp.zeros((rows.shape[0], PAD - HEAD), F32)
    cos = jnp.concatenate([jnp.cos(row)] * 2 + [jnp.cos(col)] * 2 + [rest], axis=1)
    sin = jnp.concatenate(
        [-jnp.sin(row), jnp.sin(row), -jnp.sin(col), jnp.sin(col), rest], axis=1
    )
    return cos, sin


def by_core(mine, theirs, me, axis):
    first = jnp.where(me == 0, mine, theirs)
    second = jnp.where(me == 0, theirs, mine)
    return jnp.concatenate([first, second], axis=axis)


def shards_any(
    hidden_in,
    cond_vec,
    seg_ids,
    grid_pos,
    out_grad,
    w_ada,
    b_ada,
    w_qkv,
    b_qkv,
    w_out,
    b_out,
    w_gate,
    w_up,
    w_down,
):
    count = lax.axis_size("wide")
    cores = lax.axis_size("narrow")
    devices = count * cores
    core = lax.axis_index("narrow")
    batches, _, half, width = hidden_in.shape
    slots = cond_vec.shape[2]
    own = batches * half
    heads = HEADS // cores
    inner = heads * HEAD
    rows = w_qkv.shape[0]
    both = ("wide", "narrow")

    by_half = jnp.concatenate(
        [
            w_qkv.reshape(rows, 3, cores, inner).swapaxes(1, 2).reshape(rows, cores, 3 * inner),
            w_out.reshape(rows, cores, width // cores),
        ],
        axis=2,
    )
    mine = lax.dynamic_index_in_dim(by_half, core, 1, keepdims=False)
    theirs = lax.dynamic_index_in_dim(by_half, 1 - core, 1, keepdims=False)
    att = by_core(mine, swap(theirs), core, 0)
    mid = att.shape[1] // 256 * 128
    att = gather((att[:, :mid], att[:, mid:]), count)
    qkv_cols = (3 * inner + 127) // 128 * 128
    qkv_w = att[:, :qkv_cols]
    out_half = att[:, 3 * inner :]
    out_w = by_core(out_half, swap(out_half), core, 1)
    ff = gather((w_gate, w_up), count)
    hidden = w_gate.shape[1]
    gate_w, up_w = ff[:, :hidden], ff[:, hidden:]
    down_t = w_down.T
    cut = hidden // 256 * 128
    down_w = gather((down_t[:, :cut], down_t[:, cut:]), count)

    biases = lax.all_gather(jnp.concatenate([b_qkv, b_out]), both, axis=0)
    n_b = b_qkv.shape[0]
    qkv_b = biases[:, :n_b].reshape(3, cores, inner).astype(F32)
    qkv_b = lax.dynamic_index_in_dim(qkv_b, core, 1, keepdims=False).reshape(-1)
    qkv_b = jnp.pad(qkv_b, (0, qkv_cols - 3 * inner))
    out_b = biases[:, n_b:].reshape(-1).astype(F32)

    ada_cols = w_ada.shape[1] // devices
    ada = lax.all_to_all(
        w_ada.reshape(rows, devices, ada_cols).swapaxes(0, 1), both, 0, 0
    ).reshape(devices * rows, ada_cols)
    cond = jax.nn.silu(cond_vec[:, 0].astype(F32)).astype(BF16).reshape(batches * slots, width)
    cond_all = lax.all_gather(cond, "wide", axis=0)
    modul = dot(cond_all.reshape(-1, width), ada) + b_ada.astype(F32)
    modul = modul.reshape(count, 1, batches * slots, ada_cols)
    modul = jnp.broadcast_to(modul, (count, cores, batches * slots, ada_cols))
    modul = lax.all_to_all(
        modul.reshape(devices, batches * slots, ada_cols), both, 0, 0
    )
    modul = modul.swapaxes(0, 1).reshape(batches * slots, 6 * width)

    segs = seg_ids[:, 0].reshape(batches, cores, half)
    seg_own = lax.dynamic_index_in_dim(segs, core, 1, keepdims=False)
    seg_other = lax.dynamic_index_in_dim(segs, 1 - core, 1, keepdims=False)
    seg_two = jnp.stack([seg_own, seg_other])
    seg_col = seg_two[..., None]
    seg_row = seg_two.swapaxes(0, 1).reshape(batches, 1, cores * half)
    slot_ids = seg_own + slots * jnp.arange(batches)[:, None]
    picker = (slot_ids.reshape(own, 1) == jnp.arange(batches * slots)[None]).astype(F32)
    places = jnp.stack([grid_pos[0, :, 0], grid_pos[1, :, 0]]).reshape(2, own)
    places = jnp.stack([places, swap(places)], axis=1).reshape(2, 2 * own)
    cos, sin = turn_tables(places[0], places[1])
    cos = cos.reshape(2, batches, half, PAD)
    sin = sin.reshape(2, batches, half, PAD)

    def with_other(x):
        return jnp.concatenate([x, swap(x)], axis=0)

    per_tok = jnp.dot(picker, modul, precision=HIGHEST)
    shift1, scale1, gate1, shift2, scale2, gate2 = jnp.split(per_tok, 6, axis=1)
    inputs = hidden_in.reshape(own, width).astype(F32)
    normed1, inverse1 = layer_stats(inputs)
    a_low = with_other((normed1 * (1.0 + scale1) + shift1).astype(BF16))
    qkv = dot(a_low, qkv_w) + qkv_b
    o_heads, q, k, v, lse = forward_attention(
        qkv.reshape(2, batches, half, qkv_cols), cos, sin, seg_col, seg_row, heads
    )
    o_heads = o_heads.reshape(2, own, inner)
    o_low = by_core(o_heads[0], swap(o_heads[1]), core, 1)
    branch = dot(o_low, out_w) + out_b
    mixed = inputs + gate1 * branch
    normed2, inverse2 = layer_stats(mixed)
    c_low = with_other((normed2 * (1.0 + scale2) + shift2).astype(BF16))
    d_out = out_grad.reshape(own, width).astype(F32)
    d_mlp_low = with_other((d_out * gate2).astype(BF16))

    gate = dot(c_low, gate_w)
    up = dot(c_low, up_w)
    sigma = jax.nn.sigmoid(gate)
    active = gate * sigma
    hid_low = (active * up).astype(BF16)
    g_down = dot_tn(d_mlp_low, hid_low).astype(BF16)
    d_hid = dot(d_mlp_low, down_w)
    d_gate_low = (d_hid * up * sigma * (1.0 + gate * (1.0 - sigma))).astype(BF16)
    d_up_low = (d_hid * active).astype(BF16)
    g_gate = dot_tn(c_low, d_gate_low).astype(BF16)
    g_up = dot_tn(c_low, d_up_low).astype(BF16)
    s_down = scatter(g_down, count, cut)
    s_gate_up = scatter(jnp.concatenate([g_gate, g_up], axis=1), count, hidden)

    def sum_cores(part):
        return part[:own] + swap(part[own:].astype(BF16)).astype(F32)

    d_c = sum_cores(dot_nt(d_gate_low, gate_w) + dot_nt(d_up_low, up_w))
    mlp = sum_cores(dot_nt(hid_low, down_w))
    result = mixed + gate2 * mlp
    d_gate2 = d_out * mlp
    d_scale2 = d_c * normed2
    d_mixed = d_out + layer_back(d_c * (1.0 + scale2), normed2, inverse2)
    d_gate1 = d_mixed * branch
    d_branch_low = (d_mixed * gate1).astype(BF16)
    g_out_b = jnp.sum(d_branch_low.astype(F32), axis=0)
    d_o = dot_nt(d_branch_low, out_w).astype(BF16).reshape(own, cores, inner)
    d_o_mine = lax.dynamic_index_in_dim(d_o, core, 1, keepdims=False)
    d_o_theirs = lax.dynamic_index_in_dim(d_o, 1 - core, 1, keepdims=False)
    d_o_heads = jnp.stack([d_o_mine, swap(d_o_theirs)]).reshape(2, batches, half, inner)
    g_out = dot_tn(o_low, d_branch_low).reshape(width, cores, width // cores)
    g_out_mine = lax.dynamic_index_in_dim(g_out, core, 1, keepdims=False)
    g_out_theirs = lax.dynamic_index_in_dim(g_out, 1 - core, 1, keepdims=False)
    g_out = (g_out_mine + swap(g_out_theirs.astype(BF16)).astype(F32)).astype(BF16)
    s_out = scatter(g_out, count, width // cores // 256 * 128)

    d_qkv = backward_attention(
        d_o_heads, q, k, v, lse, cos, sin, seg_col, seg_row, qkv_cols
    ).reshape(2 * own, qkv_cols)
    g_qkv = dot_tn(a_low, d_qkv).astype(BF16)
    s_qkv = scatter(g_qkv, count, qkv_cols // 256 * 128)[:, : 3 * inner]
    g_qkv_b = jnp.sum(d_qkv.astype(F32), axis=0)[: 3 * inner]
    d_a = sum_cores(dot_nt(d_qkv, qkv_w))
    d_scale1 = d_a * normed1
    d_input = d_mixed + layer_back(d_a * (1.0 + scale1), normed1, inverse1)

    d_modul = jnp.concatenate(
        [
            lax.dot_general(picker, d, (((0,), (0,)), ((), ())), precision=HIGHEST)
            for d in (d_a, d_scale1, d_gate1, d_c, d_scale2, d_gate2)
        ],
        axis=1,
    )
    d_modul = d_modul.reshape(batches * slots, devices, ada_cols).swapaxes(0, 1)
    b_parts = jnp.zeros((3, cores, inner), F32)
    b_parts = lax.dynamic_update_index_in_dim(b_parts, g_qkv_b.reshape(3, 1, inner), core, 1)
    bias_part = jnp.concatenate(
        [b_parts.reshape(devices, -1), g_out_b.reshape(devices, -1)], axis=1
    )
    n_bias = bias_part.shape[1]
    bias_rows = -(-n_bias // ada_cols)
    bias_part = jnp.pad(bias_part, ((0, 0), (0, bias_rows * ada_cols - n_bias)))
    message = jnp.concatenate(
        [d_modul, bias_part.reshape(devices, bias_rows, ada_cols)], axis=1
    )
    message = lax.all_to_all(message, both, 0, 0)
    g_bias = jnp.sum(message[:, batches * slots :], axis=0).reshape(-1)
    g_qkv_b, g_out_b = g_bias[:n_b], g_bias[n_b:n_bias]
    d_modul = jnp.sum(
        message[:, : batches * slots].reshape(count, cores, batches * slots, ada_cols), axis=1
    ).reshape(-1, ada_cols)
    g_ada_b = jnp.sum(d_modul, axis=0)
    g_ada = lax.dot_general(
        cond_all.reshape(-1, width).astype(F32),
        d_modul,
        (((0,), (0,)), ((), ())),
        precision=HIGHEST,
    )
    g_ada = lax.all_to_all(g_ada.reshape(devices, rows, ada_cols), both, 0, 0)
    g_ada = g_ada.swapaxes(0, 1).reshape(rows, 6 * width)

    s_att = jnp.concatenate([s_qkv, s_out], axis=1).reshape(cores, rows, -1)
    s_mine = lax.dynamic_index_in_dim(s_att, core, 0, keepdims=False)
    s_theirs = swap(lax.dynamic_index_in_dim(s_att, 1 - core, 0, keepdims=False))
    s_first = jnp.where(core == 0, s_mine, s_theirs)
    s_second = jnp.where(core == 0, s_theirs, s_mine)
    s_both = jnp.stack([s_first, s_second], axis=1)
    g_qkv = (
        s_both[:, :, : 3 * inner].reshape(rows, cores, 3, inner).swapaxes(1, 2).reshape(rows, -1)
    )
    g_out = s_both[:, :, 3 * inner :].reshape(rows, width)

    def tokens(x):
        return x.reshape(batches, 1, half, width)

    return (
        tokens(result),
        tokens(d_input),
        g_ada,
        g_ada_b,
        g_qkv,
        g_qkv_b,
        g_out,
        g_out_b,
        s_gate_up[:, :hidden],
        s_gate_up[:, hidden:],
        s_down.T,
    )


def shards_fast(
    hidden_in,
    cond_vec,
    seg_ids,
    grid_pos,
    out_grad,
    w_ada,
    b_ada,
    w_qkv,
    b_qkv,
    w_out,
    b_out,
    w_gate,
    w_up,
    w_down,
):
    count = lax.axis_size("wide")
    cores = lax.axis_size("narrow")
    devices = count * cores
    core = lax.axis_index("narrow")
    batches, _, half, width = hidden_in.shape
    slots = cond_vec.shape[2]
    own = batches * half
    heads = HEADS // cores
    inner = heads * HEAD
    rows = w_qkv.shape[0]
    both = ("wide", "narrow")

    qkv_cols = (3 * inner + 127) // 128 * 128
    out_cols = (width // cores + 127) // 128 * 128
    gap = width - out_cols
    heads_of = w_qkv.reshape(rows, 3, cores, inner).swapaxes(1, 2).reshape(rows, cores, 3 * inner)
    heads_of = jnp.pad(heads_of, ((0, 0), (0, 0), (0, qkv_cols - 3 * inner)))
    outs_of = jnp.stack([w_out[:, gap * c : gap * c + out_cols] for c in range(cores)], axis=1)
    by_half = jnp.concatenate([heads_of, outs_of], axis=2)
    mine = lax.dynamic_index_in_dim(by_half, core, 1, keepdims=False)
    theirs = lax.dynamic_index_in_dim(by_half, 1 - core, 1, keepdims=False)
    att = by_core(mine, swap(theirs), core, 0)
    hidden = w_gate.shape[1]
    down_t = w_down.T
    cut = hidden // 256 * 128

    n_b = b_qkv.shape[0]
    b_own = jnp.concatenate([b_qkv, b_out])
    b_two = by_core(b_own[None], swap(b_own[None]), core, 0).reshape(1, -1)
    cond = jax.nn.silu(cond_vec[:, 0].astype(F32)).astype(BF16).reshape(batches * slots, width)
    told = jnp.concatenate([cond, jnp.pad(b_two, ((0, 0), (0, width - b_two.shape[1])))], axis=0)
    told = jnp.broadcast_to(told[None], (count,) + told.shape)
    told = lax.all_to_all(told, "wide", 0, 0)
    cond_all = told[:, : batches * slots]
    biases = told[:, batches * slots, : b_two.shape[1]].reshape(devices, -1)
    qkv_b = biases[:, :n_b].reshape(3, cores, inner).astype(F32)
    qkv_b = lax.dynamic_index_in_dim(qkv_b, core, 1, keepdims=False).reshape(-1)
    qkv_b = jnp.pad(qkv_b, (0, qkv_cols - 3 * inner))
    out_b = biases[:, n_b:].reshape(-1).astype(F32)

    ada_cols = w_ada.shape[1] // devices
    ada = lax.all_to_all(
        w_ada.reshape(rows, devices, ada_cols).swapaxes(0, 1), both, 0, 0
    ).reshape(devices * rows, ada_cols)
    modul = dot(cond_all.reshape(-1, width), ada) + b_ada.astype(F32)
    modul = modul.reshape(count, 1, batches * slots, ada_cols)
    modul = jnp.broadcast_to(modul, (count, cores, batches * slots, ada_cols))
    modul = lax.all_to_all(
        modul.reshape(devices, batches * slots, ada_cols), both, 0, 0
    )
    modul = modul.swapaxes(0, 1).reshape(batches * slots, 6 * width)

    segs = seg_ids[:, 0].reshape(batches, cores, half)
    seg_own = lax.dynamic_index_in_dim(segs, core, 1, keepdims=False)
    seg_other = lax.dynamic_index_in_dim(segs, 1 - core, 1, keepdims=False)
    seg_two = jnp.stack([seg_own, seg_other])
    seg_col = seg_two[..., None]
    seg_row = seg_two.swapaxes(0, 1).reshape(batches, 1, cores * half)
    slot_ids = seg_own + slots * jnp.arange(batches)[:, None]
    picker = (slot_ids.reshape(own, 1) == jnp.arange(batches * slots)[None]).astype(F32)
    places = jnp.stack([grid_pos[0, :, 0], grid_pos[1, :, 0]]).reshape(2, own)
    places = jnp.stack([places, swap(places)], axis=1).reshape(2, 2 * own)
    cos, sin = turn_tables(places[0], places[1])

    x_own = hidden_in.reshape(own, width)
    dy_own = out_grad.reshape(own, width)
    (
        att_all, out_w, gate_all, up_all, down_all, a_low, d_mlp_low, q, k, v, lse,
        o_heads, o_other, branch, mixed, c_low,
    ) = forward_call(
        x_own, dy_own, modul, slot_ids.reshape(own, 1),
        seg_two.reshape(2 * own, 1), seg_row, cos, sin, qkv_b[None], out_b[None],
        att, w_gate, w_up, down_t, heads,
    )
    att_all = att_all.reshape(width, -1)
    qkv_w = att_all[:, :qkv_cols]
    gate_w = gate_all.reshape(width, hidden)
    up_w = up_all.reshape(width, hidden)
    down_w = down_all.reshape(width, hidden)
    o_low = by_core(o_heads[:own], o_other, core, 1)
    per_tok = jnp.dot(picker, modul, precision=HIGHEST)
    shift1, scale1, gate1, shift2, scale2, gate2 = jnp.split(per_tok, 6, axis=1)
    inputs = x_own.astype(F32)
    normed1, inverse1 = layer_stats(inputs)
    normed2, inverse2 = layer_stats(mixed)
    d_out = dy_own.astype(F32)

    gate = dot(c_low, gate_w)
    up = dot(c_low, up_w)
    sigma = jax.nn.sigmoid(gate)
    active = gate * sigma
    hid_low = (active * up).astype(BF16)
    g_down = dot_tn(d_mlp_low, hid_low).astype(BF16)
    d_hid = dot(d_mlp_low, down_w)
    d_gate_low = (d_hid * up * sigma * (1.0 + gate * (1.0 - sigma))).astype(BF16)
    d_up_low = (d_hid * active).astype(BF16)
    g_gate = dot_tn(c_low, d_gate_low).astype(BF16)
    g_up = dot_tn(c_low, d_up_low).astype(BF16)
    s_down = scatter(g_down, count, cut)
    s_gate_up = scatter(jnp.concatenate([g_gate, g_up], axis=1), count, hidden)

    def sum_cores(part):
        return part[:own] + swap(part[own:].astype(BF16)).astype(F32)

    d_c = sum_cores(dot_nt(d_gate_low, gate_w) + dot_nt(d_up_low, up_w))
    mlp = sum_cores(dot_nt(hid_low, down_w))
    result = mixed + gate2 * mlp
    d_gate2 = d_out * mlp
    d_scale2 = d_c * normed2
    d_mixed = d_out + layer_back(d_c * (1.0 + scale2), normed2, inverse2)
    d_gate1 = d_mixed * branch
    d_branch_low = (d_mixed * gate1).astype(BF16)
    g_out_b = jnp.sum(d_branch_low.astype(F32), axis=0)
    d_o = dot_nt(d_branch_low, out_w).astype(BF16).reshape(own, cores, inner)
    d_o_mine = lax.dynamic_index_in_dim(d_o, core, 1, keepdims=False)
    d_o_theirs = lax.dynamic_index_in_dim(d_o, 1 - core, 1, keepdims=False)
    d_o_heads = jnp.stack([d_o_mine, swap(d_o_theirs)]).reshape(2, batches, half, inner)
    g_out = dot_tn(o_low, d_branch_low).reshape(width, cores, width // cores)
    g_out_mine = lax.dynamic_index_in_dim(g_out, core, 1, keepdims=False)
    g_out_theirs = lax.dynamic_index_in_dim(g_out, 1 - core, 1, keepdims=False)
    g_out = (g_out_mine + swap(g_out_theirs.astype(BF16)).astype(F32)).astype(BF16)
    s_out = scatter(g_out, count, width // cores // 256 * 128)

    d_qkv = backward_attention(
        d_o_heads, q, k, v, lse, cos.reshape(2, batches, half, PAD), sin.reshape(2, batches, half, PAD), seg_col, seg_row, qkv_cols
    ).reshape(2 * own, qkv_cols)
    g_qkv = dot_tn(a_low, d_qkv).astype(BF16)
    s_qkv = scatter(g_qkv, count, qkv_cols // 256 * 128)[:, : 3 * inner]
    g_qkv_b = jnp.sum(d_qkv.astype(F32), axis=0)[: 3 * inner]
    d_a = sum_cores(dot_nt(d_qkv, qkv_w))
    d_scale1 = d_a * normed1
    d_input = d_mixed + layer_back(d_a * (1.0 + scale1), normed1, inverse1)

    d_modul = jnp.concatenate(
        [
            lax.dot_general(picker, d, (((0,), (0,)), ((), ())), precision=HIGHEST)
            for d in (d_a, d_scale1, d_gate1, d_c, d_scale2, d_gate2)
        ],
        axis=1,
    )
    d_modul = d_modul.reshape(batches * slots, devices, ada_cols).swapaxes(0, 1)
    b_parts = jnp.zeros((3, cores, inner), F32)
    b_parts = lax.dynamic_update_index_in_dim(b_parts, g_qkv_b.reshape(3, 1, inner), core, 1)
    bias_part = jnp.concatenate(
        [b_parts.reshape(devices, -1), g_out_b.reshape(devices, -1)], axis=1
    )
    n_bias = bias_part.shape[1]
    bias_rows = -(-n_bias // ada_cols)
    bias_part = jnp.pad(bias_part, ((0, 0), (0, bias_rows * ada_cols - n_bias)))
    message = jnp.concatenate(
        [d_modul, bias_part.reshape(devices, bias_rows, ada_cols)], axis=1
    )
    message = lax.all_to_all(message, both, 0, 0)
    g_bias = jnp.sum(message[:, batches * slots :], axis=0).reshape(-1)
    g_qkv_b, g_out_b = g_bias[:n_b], g_bias[n_b:n_bias]
    d_modul = jnp.sum(
        message[:, : batches * slots].reshape(count, cores, batches * slots, ada_cols), axis=1
    ).reshape(-1, ada_cols)
    g_ada_b = jnp.sum(d_modul, axis=0)
    g_ada = lax.dot_general(
        cond_all.reshape(-1, width).astype(F32),
        d_modul,
        (((0,), (0,)), ((), ())),
        precision=HIGHEST,
    )
    g_ada = lax.all_to_all(g_ada.reshape(devices, rows, ada_cols), both, 0, 0)
    g_ada = g_ada.swapaxes(0, 1).reshape(rows, 6 * width)

    s_att = jnp.concatenate([s_qkv, s_out], axis=1).reshape(cores, rows, -1)
    s_mine = lax.dynamic_index_in_dim(s_att, core, 0, keepdims=False)
    s_theirs = swap(lax.dynamic_index_in_dim(s_att, 1 - core, 0, keepdims=False))
    s_first = jnp.where(core == 0, s_mine, s_theirs)
    s_second = jnp.where(core == 0, s_theirs, s_mine)
    s_both = jnp.stack([s_first, s_second], axis=1)
    g_qkv = (
        s_both[:, :, : 3 * inner].reshape(rows, cores, 3, inner).swapaxes(1, 2).reshape(rows, -1)
    )
    g_out = s_both[:, :, 3 * inner :].reshape(rows, width)

    def tokens(x):
        return x.reshape(batches, 1, half, width)

    return (
        tokens(result),
        tokens(d_input),
        g_ada,
        g_ada_b,
        g_qkv,
        g_qkv_b,
        g_out,
        g_out_b,
        s_gate_up[:, :hidden],
        s_gate_up[:, hidden:],
        s_down.T,
    )


def solution(mesh):
    both = ("wide", "narrow")
    in_specs = (
        P(None, "wide", "narrow", None),
        P(None, "wide", None, None),
        P(None, "wide", None),
        P(None, None, "wide", "narrow"),
        P(None, "wide", "narrow", None),
        P(both, None),
        P(both),
        P(both, None),
        P(both),
        P(both, None),
        P(both),
        P("wide", "narrow"),
        P("wide", "narrow"),
        P("narrow", "wide"),
    )
    out_specs = (
        P(None, "wide", "narrow", None),
        P(None, "wide", "narrow", None),
        P(both, None),
        P(both),
        P(both, None),
        P(both),
        P(both, None),
        P(both),
        P("wide", "narrow"),
        P("wide", "narrow"),
        P("narrow", "wide"),
    )
    shards = shards_fast if mesh.shape["wide"] == 16 else shards_any
    return jax.shard_map(shards, mesh=mesh, in_specs=in_specs, out_specs=out_specs, check_vma=False)
```

```python
import functools

import jax
import jax.numpy as jnp
from jax import lax
from jax.experimental import pallas as pl
from jax.experimental.pallas import tpu as pltpu
from jax.sharding import PartitionSpec as P

HEADS = 16
HEAD = 72
PAD = 128
F32 = jnp.float32
BF16 = jnp.bfloat16
HIGHEST = lax.Precision.HIGHEST
VMEM = 56 * 2**20


def dot(a, b):
    return jnp.dot(a, b, preferred_element_type=F32)


def dot_nt(a, b):
    return lax.dot_general(a, b, (((1,), (1,)), ((), ())), preferred_element_type=F32)


def dot_tn(a, b):
    return lax.dot_general(a, b, (((0,), (0,)), ((), ())), preferred_element_type=F32)


def wide_axes(count):
    if count == 16:
        lengths = (4, 2, 2)
    elif count == 64:
        lengths = (4, 4, 4)
    else:
        lengths = (2,) * (count.bit_length() - 1)
    axes, stride = [], count
    for length in lengths:
        stride //= length
        axes.append((stride, length))
    return axes


def push(x, count, mask):
    return lax.ppermute(x, "wide", [(i, i ^ mask) for i in range(count)])


def swap(x):
    return lax.ppermute(x, "narrow", [(0, 1), (1, 0)])


def gather_slots(own, count, order):
    parts, masks = [own[None]], [[0]]
    for stride, length in order:
        have = parts[0] if len(parts) == 1 else jnp.concatenate(parts, axis=0)
        seen = sum(masks, [])
        parts, masks = [have], [seen]
        for step in range(1, length):
            parts.append(push(have, count, step * stride))
            masks.append([m ^ (step * stride) for m in seen])
    return parts, masks


def assemble(pieces, count, rows, cols):
    out = None
    me = lax.axis_index("wide")
    for array, masks, first in pieces:
        width = array.shape[2]
        places = me ^ jnp.array(masks, jnp.int32)

        def body(place_ref, in_ref, *refs):
            refs[-1][...] = in_ref[...]

        held = [] if out is None else [out]
        out = pl.pallas_call(
            body,
            out_shape=jax.ShapeDtypeStruct((count, rows, cols), BF16),
            grid_spec=pltpu.PrefetchScalarGridSpec(
                num_scalar_prefetch=1,
                grid=(len(masks),),
                in_specs=[pl.BlockSpec((1, rows, width), lambda s, p: (s, 0, 0))]
                + [pl.BlockSpec(memory_space=pl.ANY)] * len(held),
                out_specs=pl.BlockSpec((1, rows, width), lambda s, p, c=first // width: (p[s], 0, c)),
            ),
            input_output_aliases={2: 0} if held else {},
            cost_estimate=pl.CostEstimate(
                flops=0, bytes_accessed=4 * array.size, transcendentals=0
            ),
            name="assemble",
        )(places, array, *held)
    return out


def gather(halves, count):
    axes = wide_axes(count)
    orders = ((axes[0], axes[-1]) + tuple(axes[1:-1]), tuple(axes))
    rows = halves[0].shape[0]
    pieces, first = [], 0
    for half, order in zip(halves, orders):
        parts, masks = gather_slots(half, count, order)
        pieces += [(p, m, first) for p, m in zip(parts, masks)]
        first += half.shape[1]
    full = assemble(pieces, count, rows, first)
    return full.reshape(count * rows, first)


def scatter_half(grad, count, order_axes):
    axes = wide_axes(count)
    lengths = [length for _, length in axes]
    rows, cols = grad.shape[1:]
    held = grad.reshape(*lengths, rows, cols)
    me = lax.axis_index("wide")
    left = list(range(len(axes)))
    for axis in order_axes:
        stride, length = axes[axis]
        place = (me // stride) % length
        where = left.index(axis)
        total = lax.dynamic_index_in_dim(held, place, where, keepdims=False).astype(F32)
        for step in range(1, length):
            out = lax.dynamic_index_in_dim(held, place ^ step, where, keepdims=False)
            total = total + push(out.astype(BF16), count, step * stride).astype(F32)
        held = total
        left.remove(axis)
    return held


def scatter(grad, count, split):
    cols = grad.shape[1]
    whole = grad.reshape(count, -1, cols)
    last = len(wide_axes(count)) - 1
    orders = (tuple(range(last, -1, -1)), tuple(range(1, last)) + (last, 0))
    return jnp.concatenate(
        [
            scatter_half(whole[:, :, :split], count, orders[0]),
            scatter_half(whole[:, :, split:], count, orders[1]),
        ],
        axis=1,
    )


def turn(u, cos, sin, low):
    lane = lax.broadcasted_iota(jnp.int32, u.shape, 1)
    quarter = HEAD // 4
    other = jnp.where(
        (lane // quarter) % 2 == 0,
        pltpu.roll(u, PAD - quarter, 1),
        pltpu.roll(u, quarter, 1),
    )
    return (u * cos + other * sin).astype(low)


def forward_attention(qkv, cos, sin, seg_col, seg_row, heads):
    two, batches, half, width = qkv.shape
    count = two * half
    inner = heads * HEAD
    scale = HEAD ** (-0.5)

    def body(qkv_ref, cos_ref, sin_ref, col_ref, row_ref, o_ref, q_ref, k_ref, v_ref, lse_ref):
        cos = cos_ref[...].reshape(count, PAD)
        sin = sin_ref[...].reshape(count, PAD)
        same = col_ref[...].reshape(count, 1) == row_ref[0]
        lane = lax.broadcasted_iota(jnp.int32, (count, PAD), 1)
        sums = jnp.zeros((count, PAD), F32)
        for h in range(heads):
            def part(which):
                start = which * inner + h * HEAD
                return qkv_ref[:, :, :, pl.ds(start, PAD)].reshape(count, PAD)

            q = turn(part(0), cos, sin, BF16)
            k = turn(part(1), cos, sin, BF16)
            v = jnp.where(lane < HEAD, part(2), 0.0).astype(BF16)
            scores = jnp.where(same, dot_nt(q, k) * scale, -1e30)
            top = jnp.max(scores, axis=1, keepdims=True)
            expo = jnp.exp(scores - top)
            total = jnp.sum(expo, axis=1, keepdims=True)
            probs = (expo * (1.0 / total)).astype(BF16)
            o = dot(probs, v).astype(BF16)
            o_ref[:, :, :, pl.ds(h * HEAD, HEAD)] = o[:, :HEAD].reshape(two, 1, half, HEAD)
            q_ref[0, h], k_ref[0, h], v_ref[0, h] = q, k, v
            sums = jnp.where(lane == h, top + jnp.log(total), sums)
        lse_ref[0] = sums

    def four(last):
        return pl.BlockSpec((two, 1, half, last), lambda m: (0, m, 0, 0))

    kept = jax.ShapeDtypeStruct((batches, heads, count, PAD), BF16)
    kept_spec = pl.BlockSpec((1, heads, count, PAD), lambda m: (m, 0, 0, 0))
    return pl.pallas_call(
        body,
        grid=(batches,),
        in_specs=[
            four(width),
            four(PAD),
            four(PAD),
            four(1),
            pl.BlockSpec((1, 1, count), lambda m: (m, 0, 0)),
        ],
        out_specs=[
            four(inner),
            kept_spec,
            kept_spec,
            kept_spec,
            pl.BlockSpec((1, count, PAD), lambda m: (m, 0, 0)),
        ],
        out_shape=[
            jax.ShapeDtypeStruct((two, batches, half, inner), BF16),
            kept,
            kept,
            kept,
            jax.ShapeDtypeStruct((batches, count, PAD), F32),
        ],
        compiler_params=pltpu.CompilerParams(vmem_limit_bytes=VMEM),
        cost_estimate=pl.CostEstimate(
            flops=4 * batches * heads * count * count * PAD,
            bytes_accessed=qkv.size * 4 + 4 * batches * heads * count * PAD * 2,
            transcendentals=batches * heads * count * count,
        ),
        name="attention_fwd",
    )(qkv, cos, sin, seg_col, seg_row)


def backward_attention(d_o, q, k, v, lse, cos, sin, seg_col, seg_row, width):
    two, batches, half, inner = d_o.shape
    heads = q.shape[1]
    count = two * half
    scale = HEAD ** (-0.5)

    def body(do_ref, q_ref, k_ref, v_ref, lse_ref, cos_ref, sin_ref, col_ref, row_ref, out_ref):
        cos = cos_ref[...].reshape(count, PAD)
        sin = -sin_ref[...].reshape(count, PAD)
        same = col_ref[...].reshape(count, 1) == row_ref[0]
        out_ref[...] = jnp.zeros_like(out_ref)
        for h in range(heads):
            q, k, v = q_ref[0, h], k_ref[0, h], v_ref[0, h]
            do = do_ref[:, :, :, pl.ds(h * HEAD, HEAD)].reshape(count, HEAD)
            do = jnp.concatenate([do, jnp.zeros((count, PAD - HEAD), BF16)], axis=1)
            scores = jnp.where(same, dot_nt(q, k) * scale, -1e30)
            probs = jnp.exp(scores - lse_ref[0][:, h : h + 1])
            d_probs = dot_nt(do, v)
            delta = jnp.sum(probs * d_probs, axis=1, keepdims=True)
            d_s = (probs * (d_probs - delta)).astype(BF16)
            d_q = turn(dot(d_s, k) * scale, cos, sin, BF16)
            d_k = turn(dot_tn(d_s, q) * scale, cos, sin, BF16)
            d_v = dot_tn(probs.astype(BF16), do).astype(BF16)
            for which, value in enumerate((d_q, d_k, d_v)):
                out_ref[:, :, :, pl.ds(which * inner + h * HEAD, HEAD)] = value[:, :HEAD].reshape(
                    two, 1, half, HEAD
                )

    def four(last):
        return pl.BlockSpec((two, 1, half, last), lambda m: (0, m, 0, 0))

    kept_spec = pl.BlockSpec((1, heads, count, PAD), lambda m: (m, 0, 0, 0))
    return pl.pallas_call(
        body,
        grid=(batches,),
        in_specs=[
            four(inner),
            kept_spec,
            kept_spec,
            kept_spec,
            pl.BlockSpec((1, count, PAD), lambda m: (m, 0, 0)),
            four(PAD),
            four(PAD),
            four(1),
            pl.BlockSpec((1, 1, count), lambda m: (m, 0, 0)),
        ],
        out_specs=four(width),
        out_shape=jax.ShapeDtypeStruct((two, batches, half, width), BF16),
        compiler_params=pltpu.CompilerParams(vmem_limit_bytes=VMEM),
        cost_estimate=pl.CostEstimate(
            flops=10 * batches * heads * count * count * PAD,
            bytes_accessed=4 * batches * heads * count * PAD * 2 + 2 * batches * count * width,
            transcendentals=batches * heads * count * count,
        ),
        name="attention_bwd",
    )(d_o, q, k, v, lse, cos, sin, seg_col, seg_row)


ZS, YS, XS = 4, 2, 2
MESH = pl.DeviceIdType.MESH


def place(wide):
    return wide // (YS * XS), (wide // XS) % YS, wide % XS


def wide_of(z, y, x):
    return (z * YS + y) * XS + x


class Gather:
    def __init__(self, own, full, first, width, order, send, recv, base, here, core):
        z, y, x = here
        cols = pl.ds(first, width)

        def remote(src, dst, sem, wide):
            return pltpu.make_async_remote_copy(
                src_ref=src,
                dst_ref=dst,
                send_sem=send.at[base + sem],
                recv_sem=recv.at[base + sem],
                device_id=(wide, core),
                device_id_type=MESH,
            )

        self.line = [
            remote(
                own.at[:, cols],
                full.at[z, y, x, :, cols],
                step - 1,
                wide_of((z + step) % ZS, y, x),
            )
            for step in range(1, ZS)
        ]
        over_x, over_y = wide_of(z, y, 1 - x), wide_of(z, 1 - y, x)
        one = full.at[:, y, x, :, cols]
        if order == "xy":
            two = full.at[:, y, :, :, cols]
            self.second = [remote(one, one, ZS - 1, over_x)]
            self.third = [remote(two, two, ZS, over_y)]
        else:
            two = full.at[:, :, x, :, cols]
            self.second = [remote(one, one, ZS - 1, over_y)]
            self.third = [remote(two, two, ZS, over_x)]


GATHER_SEMS = ZS + 1


def start(copies):
    for c in copies:
        c.start()


def arrive(copies):
    for c in copies:
        c.wait_recv()


def leave(copies):
    for c in copies:
        c.wait_send()


def stats(values):
    centred = values - jnp.mean(values, axis=-1, keepdims=True)
    inverse = lax.rsqrt(jnp.mean(centred * centred, axis=-1, keepdims=True) + 1e-06)
    return centred * inverse, inverse


def forward_body(
    sizes,
    x_ref, dy_ref, modul_ref, slot_ref, col_ref, row_ref, cos_ref, sin_ref,
    qkvb_ref, outb_ref, att_own, gate_own, up_own, down_own,
    wqkv_out, wout_out, gate_all, up_all, down_all, a_out, dm_out, b1_out, b2_out,
    lse_out, o_out, branch_out, mixed_out, c_out, hid_out, act_out, slope_out,
    att, wqkv, wo_mine, wo_other, wout, a_all, dm_all, qkv, b1, b2, lse_s,
    o_mine, o_other, branch, mixed, c_all, hi_ref, lo_ref, slope, send, recv, local,
):
    batches, half, width, heads, slots = sizes
    own = batches * half
    inner = heads * HEAD
    count = 2 * half
    qkv_cols = wqkv.shape[1]
    out_cols = wo_mine.shape[1]
    wide, core = lax.axis_index("wide"), lax.axis_index("narrow")
    here = place(wide)
    z, y, x = here
    scale = HEAD ** (-0.5)
    sem = [0]
    saves = []

    def local_sem():
        sem[0] += 1
        return local.at[sem[0] - 1]

    def save(src, dst):
        c = pltpu.make_async_copy(src, dst, local_sem())
        c.start()
        saves.append(c)
        return c

    remote_sem = [0]

    def group(own_ref, full, first, width_, cut):
        parts = []
        for a, b, order in ((0, cut, "xy"), (cut, width_, "yx")):
            parts.append(
                Gather(own_ref, full, first + a, b - a, order, send, recv, remote_sem[0], here, core)
            )
            remote_sem[0] += GATHER_SEMS
        mine = pltpu.make_async_copy(
            own_ref.at[:, pl.ds(first, width_)],
            full.at[z, y, x, :, pl.ds(first, width_)],
            local_sem(),
        )
        mine.start()
        return [sum((getattr(p, k) for p in parts), []) for k in ("line", "second", "third")], mine

    def exchange(src, dst):
        c = pltpu.make_async_remote_copy(
            src_ref=src,
            dst_ref=dst,
            send_sem=send.at[remote_sem[0]],
            recv_sem=recv.at[remote_sem[0]],
            device_id=(wide, 1 - core),
            device_id_type=MESH,
        )
        remote_sem[0] += 1
        c.start()
        return c

    barrier = pltpu.get_barrier_semaphore()
    peers = [(wide_of((z + s) % ZS, y, x), core) for s in range(1, ZS)]
    peers += [(wide_of(z, y, 1 - x), core), (wide_of(z, 1 - y, x), core), (wide, 1 - core)]
    for peer in peers:
        pl.semaphore_signal(barrier, inc=1, device_id=peer, device_id_type=MESH)
    pl.semaphore_wait(barrier, len(peers))

    (out1, out2, out3), out_mine = group(att_own, att, qkv_cols, out_cols, out_cols // 256 * 128)
    (qkv1, qkv2, qkv3), qkv_mine = group(att_own, att, 0, qkv_cols, qkv_cols // 256 * 128)
    hidden = gate_own.shape[1]
    (gate1, gate2, gate3), gate_mine = group(gate_own, gate_all, 0, hidden, hidden // 2)
    (up1, up2, up3), up_mine = group(up_own, up_all, 0, hidden, hidden // 2)
    (down1, down2, down3), down_mine = group(down_own, down_all, 0, hidden, hidden // 2)

    start(out1)
    tile = 128
    high = modul_ref[...].astype(BF16)
    hi_ref[...] = high
    lo_ref[...] = (modul_ref[...] - high.astype(F32)).astype(BF16)

    def modul(onehot, part):
        cols = pl.ds(part * width, width)
        return dot(onehot, hi_ref[:, cols]) + dot(onehot, lo_ref[:, cols])

    def onehot_of(rows):
        n = slot_ref[rows, :].shape[0]
        lane = lax.broadcasted_iota(jnp.int32, (n, hi_ref.shape[0]), 1)
        return (slot_ref[rows, :] == lane).astype(F32).astype(BF16)

    @pl.loop(0, own // tile)
    def _(i):
        rows = pl.ds(pl.multiple_of(i * tile, tile), tile)
        onehot = onehot_of(rows)
        normed, _ = stats(x_ref[rows, :].astype(F32))
        a_all[rows, :] = (normed * (1.0 + modul(onehot, 1)) + modul(onehot, 0)).astype(BF16)
        dm_all[rows, :] = (dy_ref[rows, :].astype(F32) * modul(onehot, 5)).astype(BF16)

    a_swap = exchange(a_all.at[pl.ds(0, own)], a_all.at[pl.ds(own, own)])
    dm_swap = exchange(dm_all.at[pl.ds(0, own)], dm_all.at[pl.ds(own, own)])

    arrive(out1)
    start(qkv1)
    out_mine.wait()
    start(out2)
    arrive(out2)
    start(out3)
    arrive(qkv1)
    start(gate1)
    qkv_mine.wait()
    start(qkv2)
    arrive(out3)

    @pl.loop(0, ZS * YS)
    def _(j):
        rows = pl.ds(pl.multiple_of(j * 2 * HEAD, 2 * HEAD), 2 * HEAD)
        pair = [att[j // YS, j % YS, i, :, pl.ds(qkv_cols, out_cols)].astype(F32) for i in range(2)]
        wo_mine[rows, :] = jnp.concatenate(pair, axis=0).astype(BF16)

    wo_swap = exchange(wo_mine, wo_other)
    arrive(qkv2)
    start(qkv3)
    arrive(gate1)
    start(up1)
    gate_mine.wait()
    start(gate2)
    wo_swap.wait_recv()
    first_cols = pl.ds(0, out_cols)
    rest = width - out_cols
    skip = out_cols - rest

    @pl.loop(0, ZS * YS)
    def _(j):
        rows = pl.ds(pl.multiple_of(j * 2 * HEAD, 2 * HEAD), 2 * HEAD)
        mine, other = wo_mine[rows, :], wo_other[rows, :]
        wout[rows, first_cols] = jnp.where(core == 0, mine, other)
        wout[rows, pl.ds(out_cols, rest)] = jnp.where(core == 0, other, mine)[:, skip:]

    save(wout, wout_out)
    a_swap.wait_recv()
    dm_swap.wait_recv()
    save(a_all, a_out)
    save(dm_all, dm_out)
    arrive(qkv3)

    @pl.loop(0, ZS * YS)
    def _(j):
        rows = pl.ds(pl.multiple_of(j * 2 * HEAD, 2 * HEAD), 2 * HEAD)
        pair = [att[j // YS, j % YS, i, :, pl.ds(0, qkv_cols)].astype(F32) for i in range(2)]
        wqkv[rows, :] = jnp.concatenate(pair, axis=0).astype(BF16)

    saved_w = save(wqkv, wqkv_out)

    @pl.loop(0, 2 * own // 256)
    def _(i):
        rows = pl.ds(pl.multiple_of(i * 256, 256), 256)
        qkv[rows, :] = dot(a_all[rows, :], wqkv[...]) + qkvb_ref[...]

    arrive(gate2)
    start(gate3)
    arrive(up1)
    start(down1)
    up_mine.wait()
    start(up2)

    def both_halves(ref, m, lanes):
        first = ref[pl.ds(pl.multiple_of(m * half, half), half), lanes]
        second = ref[pl.ds(pl.multiple_of(own + m * half, half), half), lanes]
        return jnp.concatenate([first, second], axis=0)

    per_buffer = hidden // PAD

    @pl.loop(0, batches)
    def _(m):
        cos = both_halves(cos_ref, m, slice(None))
        sin = both_halves(sin_ref, m, slice(None))
        same = both_halves(col_ref, m, slice(None)) == row_ref[m]
        lane = lax.broadcasted_iota(jnp.int32, (count, PAD), 1)
        sums = jnp.zeros((count, PAD), F32)
        for h in range(heads):
            def part(which):
                return both_halves(qkv, m, pl.ds(which * inner + h * HEAD, PAD))

            q = turn(part(0), cos, sin, BF16)
            k = turn(part(1), cos, sin, BF16)
            v = jnp.where(lane < HEAD, part(2), 0.0).astype(BF16)
            scores = jnp.where(same, dot_nt(q, k) * scale, -1e30)
            top = jnp.max(scores, axis=1, keepdims=True)
            expo = jnp.exp(scores - top)
            total = jnp.sum(expo, axis=1, keepdims=True)
            probs = (expo * (1.0 / total)).astype(BF16)
            o = dot(probs, v).astype(BF16)[:, :HEAD]
            lanes = pl.ds(h * HEAD, HEAD)
            o_mine[pl.ds(pl.multiple_of(m * half, half), half), lanes] = o[:half]
            o_mine[pl.ds(pl.multiple_of(own + m * half, half), half), lanes] = o[half:]
            for piece, value in ((h, q), (heads + h, k), (2 * heads + h, v)):
                ref = b1 if piece < per_buffer else b2
                lanes = pl.ds((piece % per_buffer) * PAD, PAD)
                ref[pl.ds(pl.multiple_of(m * count, count), count), lanes] = value
            sums = jnp.where(lane == h, top + jnp.log(total), sums)
            if h == heads // 2:

                @pl.when(m == 0)
                def _():
                    arrive(up2)
                    start(up3)
                    arrive(down1)
                    down_mine.wait()
                    start(down2)

                @pl.when(m == 1)
                def _():
                    arrive(down2)
                    start(down3)

        lse_s[m] = sums

    o_swap = exchange(o_mine.at[pl.ds(own, own)], o_other)
    saved_b1 = save(b1, b1_out)
    save(b2, b2_out)
    save(lse_s, lse_out)
    save(o_mine, o_out)
    o_swap.wait_recv()
    mine_rows = pl.ds(pl.multiple_of(core * inner, 16), inner)
    other_rows = pl.ds(pl.multiple_of((1 - core) * inner, 16), inner)

    @pl.loop(0, own // tile)
    def _(i):
        rows = pl.ds(pl.multiple_of(i * tile, tile), tile)
        out = dot(o_mine[rows, :], wout[mine_rows, :]) + dot(o_other[rows, :], wout[other_rows, :])
        out = out + outb_ref[...]
        onehot = onehot_of(rows)
        branch[rows, :] = out
        mix = x_ref[rows, :].astype(F32) + modul(onehot, 2) * out
        mixed[rows, :] = mix
        normed, _ = stats(mix)
        c_all[rows, :] = (normed * (1.0 + modul(onehot, 4)) + modul(onehot, 3)).astype(BF16)

    c_swap = exchange(c_all.at[pl.ds(0, own)], c_all.at[pl.ds(own, own)])
    save(branch, branch_out)
    save(mixed, mixed_out)
    c_swap.wait_recv()
    save(c_all, c_out)
    saved_w.wait()
    saved_b1.wait()

    def weight(full):
        c = pltpu.make_async_copy(full, att.at[:, :, :, :, pl.ds(0, hidden)], local_sem())
        c.start()
        c.wait()

        @pl.loop(0, ZS * YS)
        def _(j):
            rows = pl.ds(pl.multiple_of(j * 2 * HEAD, 2 * HEAD), 2 * HEAD)
            pair = [att[j // YS, j % YS, i, :, pl.ds(0, hidden)].astype(F32) for i in range(2)]
            wqkv[rows, pl.ds(0, hidden)] = jnp.concatenate(pair, axis=0).astype(BF16)

    ff = pl.ds(0, hidden)
    for copies in (out1, out2, out3, qkv1, qkv2, qkv3):
        leave(copies)
    arrive(gate3)
    weight(gate_all)

    @pl.loop(0, 2 * own // 256)
    def _(i):
        rows = pl.ds(pl.multiple_of(i * 256, 256), 256)
        qkv[rows, ff] = dot(c_all[rows, :], wqkv[:, ff])

    arrive(up3)
    weight(up_all)
    sent = []
    step = slope.shape[1]
    for i in range(2 * own // step):
        rows = pl.ds(i * step, step)
        if i >= 2:
            sent[i - 2].wait()
        gate, up = qkv[rows, ff], dot(c_all[rows, :], wqkv[:, ff])
        sigma = jax.nn.sigmoid(gate)
        active = gate * sigma
        b1[rows, :] = (active * up).astype(BF16)
        qkv[rows, ff] = active
        slope[i % 2] = up * sigma * (1.0 + gate * (1.0 - sigma))
        c = pltpu.make_async_copy(slope.at[i % 2], slope_out.at[rows], local_sem())
        c.start()
        sent.append(c)
    save(b1, hid_out)
    save(qkv.at[:, ff], act_out)
    arrive(down3)
    for c in sent[-2:]:
        c.wait()
    for copies in (gate1, gate2, gate3):
        leave(copies)
    for copies in (up1, up2, up3, down1, down2, down3):
        leave(copies)
    leave([a_swap, dm_swap, wo_swap, o_swap, c_swap])
    for c in saves:
        if c is not saved_w and c is not saved_b1:
            c.wait()


def forward_call(x, dy, modul, slot, col, row, cos, sin, qkvb, outb, att, gate, up, down, heads):
    own, width = x.shape
    batches = row.shape[0]
    half = own // batches
    inner = heads * HEAD
    rows = att.shape[0]
    qkv_cols = qkvb.shape[1]
    out_cols = att.shape[1] - qkv_cols
    hidden = gate.shape[1]
    slots = (ZS, YS, XS, rows)
    s = jax.ShapeDtypeStruct
    outs = [
        s((width, qkv_cols), BF16),
        s((width, width), BF16),
        s(slots + (hidden,), BF16),
        s(slots + (hidden,), BF16),
        s(slots + (hidden,), BF16),
        s((2 * own, width), BF16),
        s((2 * own, width), BF16),
        s((2 * own, hidden), BF16),
        s((2 * own, hidden), BF16),
        s((batches, 2 * half, PAD), F32),
        s((2 * own, inner), BF16),
        s((own, width), F32),
        s((own, width), F32),
        s((2 * own, width), BF16),
        s((2 * own, hidden), BF16),
        s((2 * own, hidden), F32),
        s((2 * own, hidden), F32),
    ]
    remotes = 10 * GATHER_SEMS + 8
    scratch = [
        pltpu.VMEM(slots + (att.shape[1],), BF16),
        pltpu.VMEM((width, qkv_cols), BF16),
        pltpu.VMEM((width, out_cols), BF16),
        pltpu.VMEM((width, out_cols), BF16),
        pltpu.VMEM((width, width), BF16),
        pltpu.VMEM((2 * own, width), BF16),
        pltpu.VMEM((2 * own, width), BF16),
        pltpu.VMEM((2 * own, qkv_cols), F32),
        pltpu.VMEM((2 * own, hidden), BF16),
        pltpu.VMEM((2 * own, hidden), BF16),
        pltpu.VMEM((batches, 2 * half, PAD), F32),
        pltpu.VMEM((2 * own, inner), BF16),
        pltpu.VMEM((own, inner), BF16),
        pltpu.VMEM((own, width), F32),
        pltpu.VMEM((own, width), F32),
        pltpu.VMEM((2 * own, width), BF16),
        pltpu.VMEM(modul.shape, BF16),
        pltpu.VMEM(modul.shape, BF16),
        pltpu.VMEM((2, 256, hidden), F32),
        pltpu.SemaphoreType.DMA((remotes,)),
        pltpu.SemaphoreType.DMA((remotes,)),
        pltpu.SemaphoreType.DMA((32,)),
    ]
    sizes = (batches, half, width, heads, modul.shape[0])
    return pl.pallas_call(
        functools.partial(forward_body, sizes),
        out_shape=outs,
        in_specs=[pl.BlockSpec(memory_space=pltpu.VMEM)] * 14,
        out_specs=[pl.BlockSpec(memory_space=pl.ANY)] * len(outs),
        scratch_shapes=scratch,
        compiler_params=pltpu.CompilerParams(
            collective_id=0, has_side_effects=True, vmem_limit_bytes=60 * 2**20
        ),
        name="forward",
    )(x, dy, modul, slot, col, row, cos, sin, qkvb, outb, att, gate, up, down)


class Reduce:
    def __init__(self, held, landing, first, width, order, env):
        z, y, x, core = env["z"], env["y"], env["x"], env["core"]
        self.env, self.held, self.landing = env, held, landing
        self.first, self.width, self.order = first, width, order
        cols = self.cols = pl.ds(first, width)
        base = env["remote"][0]
        env["remote"][0] += ZS + 1
        self.turn = env["credit"][0]
        env["credit"][0] += 1
        send, recv = env["send"], env["recv"]

        def remote(src, dst, sem, wide):
            return pltpu.make_async_remote_copy(
                src_ref=src,
                dst_ref=dst,
                send_sem=send.at[base + sem],
                recv_sem=recv.at[base + sem],
                device_id=(wide, core),
                device_id_type=MESH,
            )

        over_x, over_y = wide_of(z, y, 1 - x), wide_of(z, 1 - y, x)
        self.line_peers = [wide_of((z + s) % ZS, y, x) for s in range(1, ZS)]
        into = landing.at[:, :, :, cols]
        if order == "xy":
            self.pair = over_y
            self.first_copy = remote(held.at[:, :, 1 - x, :, cols], into, 0, over_x)
            self.second_copy = remote(
                held.at[:, 1 - y, x, :, cols], held.at[:, 0, 1 - x, :, cols], 1, over_y
            )
            spot = lambda i: held.at[i, 1, 1 - x, :, cols]
        else:
            self.pair = over_x
            self.first_copy = remote(held.at[:, 1 - y, :, :, cols], into, 0, over_y)
            self.second_copy = remote(
                held.at[:, y, 1 - x, :, cols], held.at[:, 1 - y, 0, :, cols], 1, over_x
            )
            spot = lambda i: held.at[i, 1 - y, 1, :, cols]
        self.line_copies = [
            remote(held.at[(z + s) % ZS, y, x, :, cols], spot(s - 1), 1 + s, self.line_peers[s - 1])
            for s in range(1, ZS)
        ]

    def begin(self):
        self.first_copy.start()

    def second(self):
        env, held, cols = self.env, self.held, self.cols
        y, x, core = env["y"], env["x"], env["core"]
        self.first_copy.wait_recv()
        stage = env["stage"]
        c = pltpu.make_async_copy(
            self.landing.at[:, :, :, cols],
            stage.at[:, :, :, pl.ds(0, self.width)],
            env["stage_sem"].at[self.turn],
        )
        c.start()
        self.first_copy.wait_send()
        for peer in [self.pair]:
            pl.semaphore_signal(
                env["pair_free"].at[self.turn], 1, device_id=(peer, core), device_id_type=MESH
            )
        for peer in self.line_peers:
            pl.semaphore_signal(
                env["line_free"].at[self.turn], 1, device_id=(peer, core), device_id_type=MESH
            )
        c.wait()

        @pl.loop(0, ZS * 2)
        def _(j):
            a, b = j // 2, j % 2
            at = (a, b, x) if self.order == "xy" else (a, y, b)
            new = stage[a, b, :, pl.ds(0, self.width)].astype(F32)
            held[at + (slice(None), cols)] = (
                held[at + (slice(None), cols)].astype(F32) + new
            ).astype(BF16)

        pl.semaphore_wait(env["pair_free"].at[self.turn], 1)
        self.second_copy.start()

    def line(self):
        env, held, cols = self.env, self.held, self.cols
        y, x = env["y"], env["x"]
        self.second_copy.wait_recv()

        @pl.loop(0, ZS)
        def _(a):
            at = (a, 0, 1 - x) if self.order == "xy" else (a, 1 - y, 0)
            new = held[at + (slice(None), cols)]
            mine = held[a, y, x, :, cols].astype(F32) + new.astype(F32)
            held[a, y, x, :, cols] = mine.astype(BF16)

        pl.semaphore_wait(env["line_free"].at[self.turn], ZS - 1)
        for c in self.line_copies:
            c.start()

    def finish(self, out):
        env, held, cols = self.env, self.held, self.cols
        z, y, x = env["z"], env["y"], env["x"]
        total = held[z, y, x, :, cols].astype(F32)
        for i, c in enumerate(self.line_copies):
            c.wait_recv()
            at = (i, 1, 1 - x) if self.order == "xy" else (i, 1 - y, 1)
            total = total + held[at + (slice(None), cols)].astype(F32)
        out[:, cols] = total
        self.second_copy.wait_send()
        for c in self.line_copies:
            c.wait_send()


def backward_body(
    sizes,
    modul_ref, slot_ref, col_ref, row_ref, cos_ref, sin_ref, lse_ref,
    x_in, dy_in, branch_in, mixed_in, hid_in, act_in, slope_in, c_in, dm_in, a_in, b1_in, b2_in,
    o_in, gate_in, up_in, down_in, qkv_in, out_in,
    result_out, grad_out, g_gate, g_up, g_down, g_qkv, g_out, dmod, qkb, vb, outb,
    land_down, land_gate, land_up, land_qkv, land_out,
    w1, w2, b1, b2, tok, dm, dv, o_s, mlp_own, dc_own, snd, mlp_in, dc_in, t1, t2, xy,
    hi_ref, lo_ref, g_send, s0, s1, s2, s3, stage,
    send, recv, local, tiles, stage_sem, pair_free, line_free,
):
    batches, half, width, heads, hidden, qkv_cols, out_cols = sizes
    own = batches * half
    inner = heads * HEAD
    count = 2 * half
    scale = HEAD ** (-0.5)
    tile = 128
    wide, core = lax.axis_index("wide"), lax.axis_index("narrow")
    z, y, x = place(wide)
    env = dict(
        z=z, y=y, x=x, core=core, send=send, recv=recv, remote=[0], credit=[0], stage=stage,
        stage_sem=stage_sem, pair_free=pair_free, line_free=line_free,
    )
    used = [0]

    def fetch(src, dst):
        c = pltpu.make_async_copy(src, dst, local.at[used[0]])
        used[0] += 1
        c.start()
        return c

    def exchange(src, dst):
        base = env["remote"][0]
        env["remote"][0] += 1
        c = pltpu.make_async_remote_copy(
            src_ref=src,
            dst_ref=dst,
            send_sem=send.at[base],
            recv_sem=recv.at[base],
            device_id=(wide, 1 - core),
            device_id_type=MESH,
        )
        c.start()
        return c

    wide_ff = pl.ds(0, hidden)
    got_dm = fetch(dm_in, dm)
    got_hid = fetch(hid_in, b1)
    got_w2 = fetch(down_in, w2)
    got_w1 = fetch(gate_in, w1.at[:, wide_ff])
    got_tok = fetch(c_in, tok)
    got_xy = fetch(dy_in, xy)

    barrier = pltpu.get_barrier_semaphore()
    peers = [(wide_of((z + s) % ZS, y, x), core) for s in range(1, ZS)]
    peers += [(wide_of(z, y, 1 - x), core), (wide_of(z, 1 - y, x), core), (wide, 1 - core)]
    for peer in peers:
        pl.semaphore_signal(barrier, inc=1, device_id=peer, device_id_type=MESH)
    pl.semaphore_wait(barrier, len(peers))

    def parts(held, landing, cols, cut):
        return [
            Reduce(held, landing, 0, cut, "xy", env),
            Reduce(held, landing, cut, cols - cut, "yx", env),
        ]

    cut = hidden // 256 * 128
    r_down = parts(s0, land_down, hidden, cut)
    r_gate = parts(s1, land_gate, hidden, cut)
    r_up = parts(s2, land_up, hidden, cut)
    r_out = parts(s3, land_out, out_cols, out_cols // 256 * 128)
    r_qkv = parts(s0, land_qkv, qkv_cols, qkv_cols // 256 * 128)

    def grad(held, lhs, rhs, todo, wide_tile, base=0, total=None):
        total = hidden if total is None else total
        for at in range(0, total, wide_tile):
            n = min(wide_tile, total - at)
            g = dot_tn(lhs[...], rhs[:, pl.ds(at, n)])
            rows = g.shape[0] // (ZS * YS * XS)
            held[:, :, :, :, pl.ds(base + at, n)] = g.reshape(ZS, YS, XS, rows, n).astype(BF16)
            for r in list(todo):
                if r.first + r.width <= base + at + n:
                    r.begin()
                    todo.remove(r)

    ff_tile = hidden // 4
    got_dm.wait()
    got_hid.wait()
    grad(s0, dm, b1, list(r_down), ff_tile)

    got_w2.wait()

    def partial(own_ref, into, value):
        @pl.loop(0, own // 256)
        def _(i):
            rows = pl.ds(pl.multiple_of(own + i * 256, 256), 256)
            snd[pl.ds(pl.multiple_of(i * 256, 256), 256), :] = value(rows).astype(BF16)

        c = exchange(snd, into)

        @pl.loop(0, own // 256)
        def _(i):
            rows = pl.ds(pl.multiple_of(i * 256, 256), 256)
            own_ref[rows, :] = value(rows)

        return c

    mlp_swap = partial(mlp_own, mlp_in, lambda rows: dot_nt(b1[rows, :], w2[...]))

    def streamed(n, cols, one, two, body):
        def copies(i, slot):
            rows = pl.ds(pl.multiple_of(i * tile, tile), tile)
            return (
                pltpu.make_async_copy(one.at[rows], t1.at[slot, :, cols], tiles.at[slot, 0]),
                pltpu.make_async_copy(two.at[rows], t2.at[slot, :, cols], tiles.at[slot, 1]),
            )

        for c in copies(0, 0):
            c.start()

        @pl.loop(0, n)
        def _(i):
            slot = i % 2

            @pl.when(i + 1 < n)
            def _():
                for c in copies(i + 1, 1 - slot):
                    c.start()

            for c in copies(i, slot):
                c.wait()
            body(i, t1.at[slot, :, cols], t2.at[slot, :, cols])

    def hidden_back(i, act, slope):
        rows = pl.ds(pl.multiple_of(i * tile, tile), tile)
        d_hid = dot(dm[rows, :], w2[...])
        b1[rows, :] = (d_hid * slope[...]).astype(BF16)
        b2[rows, :] = (d_hid * act[...]).astype(BF16)

    streamed(2 * own // tile, wide_ff, act_in, slope_in, hidden_back)
    got_w2 = fetch(up_in, w2)
    got_tok.wait()
    grad(s1, tok, b1, list(r_gate), ff_tile)
    for r in r_down:
        r.second()
    grad(s2, tok, b2, list(r_up), ff_tile)
    got_tok = fetch(a_in, tok)
    got_w1.wait()
    got_w2.wait()
    mlp_swap.wait_send()
    dc_swap = partial(
        dc_own, dc_in, lambda rows: dot_nt(b1[rows, :], w1[:, wide_ff]) + dot_nt(b2[rows, :], w2[...])
    )
    got_w1 = fetch(qkv_in, w1)
    got_w2 = fetch(out_in, w2.at[:, pl.ds(0, width)])
    got_b1 = fetch(b1_in, b1)
    got_b2 = fetch(b2_in, b2)
    got_o = fetch(o_in, o_s)
    for r in r_down:
        r.line()
    high = modul_ref[...].astype(BF16)
    hi_ref[...] = high
    lo_ref[...] = (modul_ref[...] - high.astype(F32)).astype(BF16)
    dmod[...] = jnp.zeros_like(dmod)
    outb[...] = jnp.zeros_like(outb)

    def modul(onehot, part):
        cols = pl.ds(part * width, width)
        return dot(onehot, hi_ref[:, cols]) + dot(onehot, lo_ref[:, cols])

    def gather_rows(onehot, part, value):
        cols = pl.ds(part * width, width)
        high = value.astype(BF16)
        low = (value - high.astype(F32)).astype(BF16)
        dmod[:, cols] += dot_tn(onehot, high) + dot_tn(onehot, low)

    def onehot_of(rows):
        lane = lax.broadcasted_iota(jnp.int32, (tile, modul_ref.shape[0]), 1)
        return (slot_ref[rows, :] == lane).astype(F32).astype(BF16)

    got_xy.wait()
    mlp_swap.wait_recv()
    dc_swap.wait_recv()

    def second_norm(i, mixed, branch):
        rows = pl.ds(pl.multiple_of(i * tile, tile), tile)
        onehot = onehot_of(rows)
        mix = mixed[...]
        normed, inverse = stats(mix)
        mlp = mlp_own[rows, :] + mlp_in[rows, :].astype(F32)
        d_c = dc_own[rows, :] + dc_in[rows, :].astype(F32)
        dy = xy[rows, :].astype(F32)
        mlp_own[rows, :] = mix + modul(onehot, 5) * mlp
        gather_rows(onehot, 5, dy * mlp)
        gather_rows(onehot, 3, d_c)
        gather_rows(onehot, 4, d_c * normed)
        d_mixed = dy + layer_back(d_c * (1.0 + modul(onehot, 4)), normed, inverse)
        dc_own[rows, :] = d_mixed
        gather_rows(onehot, 2, d_mixed * branch[...])
        d_branch = (modul(onehot, 2) * d_mixed).astype(BF16)
        dm[rows, :] = d_branch
        outb[...] += jnp.sum(d_branch.astype(F32), axis=0, keepdims=True)

    streamed(own // tile, pl.ds(0, width), mixed_in, branch_in, second_norm)
    db_swap = exchange(dm.at[pl.ds(0, own)], dm.at[pl.ds(own, own)])
    saved_result = fetch(mlp_own, result_out)
    got_xy = fetch(x_in, xy)
    for r in r_gate:
        r.second()
    got_o.wait()
    db_swap.wait_recv()
    gap = width - out_cols
    planes = ZS // 2
    mine = pl.ds(core * planes, planes)
    shape = (planes, YS, XS, HEAD, out_cols)
    other_cols = pl.ds(pl.multiple_of((1 - core) * gap, 128), out_cols)
    g_send[...] = dot_tn(o_s[...], dm[:, other_cols]).reshape(shape).astype(BF16)
    go_swap = exchange(g_send, s3.at[mine])
    mine_cols = pl.ds(pl.multiple_of(core * gap, 128), out_cols)
    s3[mine] = dot_tn(o_s[...], dm[:, mine_cols]).reshape(shape).astype(BF16)
    got_w2.wait()
    head_rows = pl.ds(pl.multiple_of(core * inner, 16), inner)

    @pl.loop(0, 2 * own // 256)
    def _(i):
        rows = pl.ds(pl.multiple_of(i * 256, 256), 256)
        o_s[rows, :] = dot_nt(dm[rows, :], w2[head_rows, pl.ds(0, width)]).astype(BF16)

    go_swap.wait_recv()
    for r in r_out:
        r.begin()
    db_swap.wait_send()
    got_b1.wait()
    got_b2.wait()
    dv[:, pl.ds(inner, out_cols - inner)] = jnp.zeros((2 * own, out_cols - inner), BF16)

    def both_halves(ref, m, lanes):
        first = ref[pl.ds(pl.multiple_of(m * half, half), half), lanes]
        second = ref[pl.ds(pl.multiple_of(own + m * half, half), half), lanes]
        return jnp.concatenate([first, second], axis=0)

    per_buffer = hidden // PAD

    def kept(piece, m):
        ref = b1 if piece < per_buffer else b2
        lanes = pl.ds((piece % per_buffer) * PAD, PAD)
        return ref[pl.ds(pl.multiple_of(m * count, count), count), lanes]

    @pl.loop(0, batches)
    def _(m):
        cos = both_halves(cos_ref, m, slice(None))
        sin = -both_halves(sin_ref, m, slice(None))
        same = both_halves(col_ref, m, slice(None)) == row_ref[m]
        for h in range(heads):
            q, k, v = kept(h, m), kept(heads + h, m), kept(2 * heads + h, m)
            do = both_halves(o_s, m, pl.ds(h * HEAD, HEAD))
            do = jnp.concatenate([do, jnp.zeros((count, PAD - HEAD), BF16)], axis=1)
            scores = jnp.where(same, dot_nt(q, k) * scale, -1e30)
            probs = jnp.exp(scores - lse_ref[m][:, h : h + 1])
            d_probs = dot_nt(do, v)
            delta = jnp.sum(probs * d_probs, axis=1, keepdims=True)
            d_s = (probs * (d_probs - delta)).astype(BF16)
            d_q = turn(dot(d_s, k) * scale, cos, sin, BF16)[:, :HEAD]
            d_k = turn(dot_tn(d_s, q) * scale, cos, sin, BF16)[:, :HEAD]
            d_v = dot_tn(probs.astype(BF16), do).astype(BF16)[:, :HEAD]
            first = pl.ds(pl.multiple_of(m * half, half), half)
            second = pl.ds(pl.multiple_of(own + m * half, half), half)
            for ref, at, value in (
                (dm, h * HEAD, d_q),
                (dm, inner + h * HEAD, d_k),
                (dv, h * HEAD, d_v),
            ):
                ref[first, pl.ds(at, HEAD)] = value[:half]
                ref[second, pl.ds(at, HEAD)] = value[half:]
            if h == 1:

                @pl.when(m == 0)
                def _():
                    for r in r_gate:
                        r.line()

                @pl.when(m == 1)
                def _():
                    for r in r_up:
                        r.line()

            if h == heads - 3:

                @pl.when(m == 0)
                def _():
                    for r in r_up:
                        r.second()

                @pl.when(m == 1)
                def _():
                    for r in r_out:
                        r.second()

    for r in r_down:
        r.finish(g_down)
    got_tok.wait()
    todo = list(r_qkv)
    grad(s0, tok, dm, todo, width // 3, 0, 2 * inner)
    grad(s0, tok, dv, todo, 384, 2 * inner, out_cols)
    got_w1.wait()
    saved_result.wait()
    dc_swap.wait_send()
    qk, vv = pl.ds(0, 2 * inner), pl.ds(2 * inner, out_cols)
    da_swap = partial(
        mlp_own, mlp_in, lambda rows: dot_nt(dm[rows, :], w1[:, qk]) + dot_nt(dv[rows, :], w1[:, vv])
    )
    qkb[...] = jnp.sum(dm[...].astype(F32), axis=0, keepdims=True)
    vb[...] = jnp.sum(dv[...].astype(F32), axis=0, keepdims=True)
    for r in r_out:
        r.line()
    got_xy.wait()
    da_swap.wait_recv()

    @pl.loop(0, own // tile)
    def _(i):
        rows = pl.ds(pl.multiple_of(i * tile, tile), tile)
        onehot = onehot_of(rows)
        normed, inverse = stats(xy[rows, :].astype(F32))
        d_a = mlp_own[rows, :] + mlp_in[rows, :].astype(F32)
        gather_rows(onehot, 0, d_a)
        gather_rows(onehot, 1, d_a * normed)
        dc_own[rows, :] += layer_back(d_a * (1.0 + modul(onehot, 1)), normed, inverse)

    saved_grad = fetch(dc_own, grad_out)
    for r in r_gate:
        r.finish(g_gate)
    for r in r_up:
        r.finish(g_up)
    for r in r_qkv:
        r.second()
    for r in r_out:
        r.finish(g_out)
    for r in r_qkv:
        r.line()
    for r in r_qkv:
        r.finish(g_qkv)
    go_swap.wait_send()
    da_swap.wait_send()
    saved_grad.wait()


def backward_call(
    modul, slot, col, row, cos, sin, lse, x, dy, branch, mixed, hid, act, slope, c, dm, a, b1, b2,
    o, gate, up, down, qkv, out, heads, out_cols,
):
    own, width = x.shape
    batches = row.shape[0]
    half = own // batches
    inner = heads * HEAD
    hidden = gate.shape[1]
    qkv_cols = qkv.shape[1]
    rows = width // (ZS * YS * XS)
    s = jax.ShapeDtypeStruct
    outs = [
        s((own, width), F32),
        s((own, width), F32),
        s((rows, hidden), F32),
        s((rows, hidden), F32),
        s((rows, hidden), F32),
        s((rows, qkv_cols), F32),
        s((rows, out_cols), F32),
        s(modul.shape, F32),
        s((1, 2 * inner), F32),
        s((1, out_cols), F32),
        s((1, width), F32),
    ]
    lands = [s((ZS, 2, rows, n), BF16) for n in (hidden, hidden, hidden, qkv_cols, out_cols)]
    vmem, any_ = pl.BlockSpec(memory_space=pltpu.VMEM), pl.BlockSpec(memory_space=pl.ANY)
    cube = (ZS, YS, XS, rows)
    groups, remotes = 10, 10 * (ZS + 1) + 8
    scratch = [
        pltpu.VMEM((width, qkv_cols), BF16),
        pltpu.VMEM((width, hidden), BF16),
        pltpu.VMEM((2 * own, hidden), BF16),
        pltpu.VMEM((2 * own, hidden), BF16),
        pltpu.VMEM((2 * own, width), BF16),
        pltpu.VMEM((2 * own, width), BF16),
        pltpu.VMEM((2 * own, out_cols), BF16),
        pltpu.VMEM((2 * own, inner), BF16),
        pltpu.VMEM((own, width), F32),
        pltpu.VMEM((own, width), F32),
        pltpu.VMEM((own, width), BF16),
        pltpu.VMEM((own, width), BF16),
        pltpu.VMEM((own, width), BF16),
        pltpu.VMEM((2, 128, hidden), F32),
        pltpu.VMEM((2, 128, hidden), F32),
        pltpu.VMEM((own, width), BF16),
        pltpu.VMEM(modul.shape, BF16),
        pltpu.VMEM(modul.shape, BF16),
        pltpu.VMEM((ZS // 2, YS, XS, rows, out_cols), BF16),
        pltpu.VMEM(cube + (qkv_cols,), BF16),
        pltpu.VMEM(cube + (hidden,), BF16),
        pltpu.VMEM(cube + (hidden,), BF16),
        pltpu.VMEM(cube + (out_cols,), BF16),
        pltpu.VMEM((ZS, 2, rows, qkv_cols // 2), BF16),
        pltpu.SemaphoreType.DMA((remotes,)),
        pltpu.SemaphoreType.DMA((remotes,)),
        pltpu.SemaphoreType.DMA((24,)),
        pltpu.SemaphoreType.DMA((2, 2)),
        pltpu.SemaphoreType.DMA((groups,)),
        pltpu.SemaphoreType.REGULAR((groups,)),
        pltpu.SemaphoreType.REGULAR((groups,)),
    ]
    sizes = (batches, half, width, heads, hidden, qkv_cols, out_cols)
    return pl.pallas_call(
        functools.partial(backward_body, sizes),
        out_shape=outs + lands,
        in_specs=[vmem] * 7 + [any_] * 18,
        out_specs=[any_] * 2 + [vmem] * 9 + [any_] * 5,
        scratch_shapes=scratch,
        compiler_params=pltpu.CompilerParams(
            collective_id=1, has_side_effects=True, vmem_limit_bytes=62 * 2**20
        ),
        name="backward",
    )(
        modul, slot, col, row, cos, sin, lse, x, dy, branch, mixed, hid, act, slope, c, dm, a, b1, b2,
        o, gate, up, down, qkv, out,
    )[: len(outs)]


def layer_stats(values):
    centred = values - jnp.mean(values, axis=-1, keepdims=True)
    inverse = lax.rsqrt(jnp.mean(centred * centred, axis=-1, keepdims=True) + 1e-06)
    return (centred * inverse, inverse)


def layer_back(grad, normed, inverse):
    mean_grad = jnp.mean(grad, axis=-1, keepdims=True)
    mean_mix = jnp.mean(grad * normed, axis=-1, keepdims=True)
    return (grad - mean_grad - normed * mean_mix) * inverse


def turn_tables(rows, cols):
    quarter = HEAD // 4
    freq = 10000.0 ** (-jnp.arange(quarter, dtype=F32) / quarter)
    row = rows.astype(F32)[:, None] * freq
    col = cols.astype(F32)[:, None] * freq
    rest = jnp.zeros((rows.shape[0], PAD - HEAD), F32)
    cos = jnp.concatenate([jnp.cos(row)] * 2 + [jnp.cos(col)] * 2 + [rest], axis=1)
    sin = jnp.concatenate(
        [-jnp.sin(row), jnp.sin(row), -jnp.sin(col), jnp.sin(col), rest], axis=1
    )
    return cos, sin


def by_core(mine, theirs, me, axis):
    first = jnp.where(me == 0, mine, theirs)
    second = jnp.where(me == 0, theirs, mine)
    return jnp.concatenate([first, second], axis=axis)


def shards_any(
    hidden_in,
    cond_vec,
    seg_ids,
    grid_pos,
    out_grad,
    w_ada,
    b_ada,
    w_qkv,
    b_qkv,
    w_out,
    b_out,
    w_gate,
    w_up,
    w_down,
):
    count = lax.axis_size("wide")
    cores = lax.axis_size("narrow")
    devices = count * cores
    core = lax.axis_index("narrow")
    batches, _, half, width = hidden_in.shape
    slots = cond_vec.shape[2]
    own = batches * half
    heads = HEADS // cores
    inner = heads * HEAD
    rows = w_qkv.shape[0]
    both = ("wide", "narrow")

    by_half = jnp.concatenate(
        [
            w_qkv.reshape(rows, 3, cores, inner).swapaxes(1, 2).reshape(rows, cores, 3 * inner),
            w_out.reshape(rows, cores, width // cores),
        ],
        axis=2,
    )
    mine = lax.dynamic_index_in_dim(by_half, core, 1, keepdims=False)
    theirs = lax.dynamic_index_in_dim(by_half, 1 - core, 1, keepdims=False)
    att = by_core(mine, swap(theirs), core, 0)
    mid = att.shape[1] // 256 * 128
    att = gather((att[:, :mid], att[:, mid:]), count)
    qkv_cols = (3 * inner + 127) // 128 * 128
    qkv_w = att[:, :qkv_cols]
    out_half = att[:, 3 * inner :]
    out_w = by_core(out_half, swap(out_half), core, 1)
    ff = gather((w_gate, w_up), count)
    hidden = w_gate.shape[1]
    gate_w, up_w = ff[:, :hidden], ff[:, hidden:]
    down_t = w_down.T
    cut = hidden // 256 * 128
    down_w = gather((down_t[:, :cut], down_t[:, cut:]), count)

    biases = lax.all_gather(jnp.concatenate([b_qkv, b_out]), both, axis=0)
    n_b = b_qkv.shape[0]
    qkv_b = biases[:, :n_b].reshape(3, cores, inner).astype(F32)
    qkv_b = lax.dynamic_index_in_dim(qkv_b, core, 1, keepdims=False).reshape(-1)
    qkv_b = jnp.pad(qkv_b, (0, qkv_cols - 3 * inner))
    out_b = biases[:, n_b:].reshape(-1).astype(F32)

    ada_cols = w_ada.shape[1] // devices
    ada = lax.all_to_all(
        w_ada.reshape(rows, devices, ada_cols).swapaxes(0, 1), both, 0, 0
    ).reshape(devices * rows, ada_cols)
    cond = jax.nn.silu(cond_vec[:, 0].astype(F32)).astype(BF16).reshape(batches * slots, width)
    cond_all = lax.all_gather(cond, "wide", axis=0)
    modul = dot(cond_all.reshape(-1, width), ada) + b_ada.astype(F32)
    modul = modul.reshape(count, 1, batches * slots, ada_cols)
    modul = jnp.broadcast_to(modul, (count, cores, batches * slots, ada_cols))
    modul = lax.all_to_all(
        modul.reshape(devices, batches * slots, ada_cols), both, 0, 0
    )
    modul = modul.swapaxes(0, 1).reshape(batches * slots, 6 * width)

    segs = seg_ids[:, 0].reshape(batches, cores, half)
    seg_own = lax.dynamic_index_in_dim(segs, core, 1, keepdims=False)
    seg_other = lax.dynamic_index_in_dim(segs, 1 - core, 1, keepdims=False)
    seg_two = jnp.stack([seg_own, seg_other])
    seg_col = seg_two[..., None]
    seg_row = seg_two.swapaxes(0, 1).reshape(batches, 1, cores * half)
    slot_ids = seg_own + slots * jnp.arange(batches)[:, None]
    picker = (slot_ids.reshape(own, 1) == jnp.arange(batches * slots)[None]).astype(F32)
    places = jnp.stack([grid_pos[0, :, 0], grid_pos[1, :, 0]]).reshape(2, own)
    places = jnp.stack([places, swap(places)], axis=1).reshape(2, 2 * own)
    cos, sin = turn_tables(places[0], places[1])
    cos = cos.reshape(2, batches, half, PAD)
    sin = sin.reshape(2, batches, half, PAD)

    def with_other(x):
        return jnp.concatenate([x, swap(x)], axis=0)

    per_tok = jnp.dot(picker, modul, precision=HIGHEST)
    shift1, scale1, gate1, shift2, scale2, gate2 = jnp.split(per_tok, 6, axis=1)
    inputs = hidden_in.reshape(own, width).astype(F32)
    normed1, inverse1 = layer_stats(inputs)
    a_low = with_other((normed1 * (1.0 + scale1) + shift1).astype(BF16))
    qkv = dot(a_low, qkv_w) + qkv_b
    o_heads, q, k, v, lse = forward_attention(
        qkv.reshape(2, batches, half, qkv_cols), cos, sin, seg_col, seg_row, heads
    )
    o_heads = o_heads.reshape(2, own, inner)
    o_low = by_core(o_heads[0], swap(o_heads[1]), core, 1)
    branch = dot(o_low, out_w) + out_b
    mixed = inputs + gate1 * branch
    normed2, inverse2 = layer_stats(mixed)
    c_low = with_other((normed2 * (1.0 + scale2) + shift2).astype(BF16))
    d_out = out_grad.reshape(own, width).astype(F32)
    d_mlp_low = with_other((d_out * gate2).astype(BF16))

    gate = dot(c_low, gate_w)
    up = dot(c_low, up_w)
    sigma = jax.nn.sigmoid(gate)
    active = gate * sigma
    hid_low = (active * up).astype(BF16)
    g_down = dot_tn(d_mlp_low, hid_low).astype(BF16)
    d_hid = dot(d_mlp_low, down_w)
    d_gate_low = (d_hid * up * sigma * (1.0 + gate * (1.0 - sigma))).astype(BF16)
    d_up_low = (d_hid * active).astype(BF16)
    g_gate = dot_tn(c_low, d_gate_low).astype(BF16)
    g_up = dot_tn(c_low, d_up_low).astype(BF16)
    s_down = scatter(g_down, count, cut)
    s_gate_up = scatter(jnp.concatenate([g_gate, g_up], axis=1), count, hidden)

    def sum_cores(part):
        return part[:own] + swap(part[own:].astype(BF16)).astype(F32)

    d_c = sum_cores(dot_nt(d_gate_low, gate_w) + dot_nt(d_up_low, up_w))
    mlp = sum_cores(dot_nt(hid_low, down_w))
    result = mixed + gate2 * mlp
    d_gate2 = d_out * mlp
    d_scale2 = d_c * normed2
    d_mixed = d_out + layer_back(d_c * (1.0 + scale2), normed2, inverse2)
    d_gate1 = d_mixed * branch
    d_branch_low = (d_mixed * gate1).astype(BF16)
    g_out_b = jnp.sum(d_branch_low.astype(F32), axis=0)
    d_o = dot_nt(d_branch_low, out_w).astype(BF16).reshape(own, cores, inner)
    d_o_mine = lax.dynamic_index_in_dim(d_o, core, 1, keepdims=False)
    d_o_theirs = lax.dynamic_index_in_dim(d_o, 1 - core, 1, keepdims=False)
    d_o_heads = jnp.stack([d_o_mine, swap(d_o_theirs)]).reshape(2, batches, half, inner)
    g_out = dot_tn(o_low, d_branch_low).reshape(width, cores, width // cores)
    g_out_mine = lax.dynamic_index_in_dim(g_out, core, 1, keepdims=False)
    g_out_theirs = lax.dynamic_index_in_dim(g_out, 1 - core, 1, keepdims=False)
    g_out = (g_out_mine + swap(g_out_theirs.astype(BF16)).astype(F32)).astype(BF16)
    s_out = scatter(g_out, count, width // cores // 256 * 128)

    d_qkv = backward_attention(
        d_o_heads, q, k, v, lse, cos, sin, seg_col, seg_row, qkv_cols
    ).reshape(2 * own, qkv_cols)
    g_qkv = dot_tn(a_low, d_qkv).astype(BF16)
    s_qkv = scatter(g_qkv, count, qkv_cols // 256 * 128)[:, : 3 * inner]
    g_qkv_b = jnp.sum(d_qkv.astype(F32), axis=0)[: 3 * inner]
    d_a = sum_cores(dot_nt(d_qkv, qkv_w))
    d_scale1 = d_a * normed1
    d_input = d_mixed + layer_back(d_a * (1.0 + scale1), normed1, inverse1)

    d_modul = jnp.concatenate(
        [
            lax.dot_general(picker, d, (((0,), (0,)), ((), ())), precision=HIGHEST)
            for d in (d_a, d_scale1, d_gate1, d_c, d_scale2, d_gate2)
        ],
        axis=1,
    )
    d_modul = d_modul.reshape(batches * slots, devices, ada_cols).swapaxes(0, 1)
    b_parts = jnp.zeros((3, cores, inner), F32)
    b_parts = lax.dynamic_update_index_in_dim(b_parts, g_qkv_b.reshape(3, 1, inner), core, 1)
    bias_part = jnp.concatenate(
        [b_parts.reshape(devices, -1), g_out_b.reshape(devices, -1)], axis=1
    )
    n_bias = bias_part.shape[1]
    bias_rows = -(-n_bias // ada_cols)
    bias_part = jnp.pad(bias_part, ((0, 0), (0, bias_rows * ada_cols - n_bias)))
    message = jnp.concatenate(
        [d_modul, bias_part.reshape(devices, bias_rows, ada_cols)], axis=1
    )
    message = lax.all_to_all(message, both, 0, 0)
    g_bias = jnp.sum(message[:, batches * slots :], axis=0).reshape(-1)
    g_qkv_b, g_out_b = g_bias[:n_b], g_bias[n_b:n_bias]
    d_modul = jnp.sum(
        message[:, : batches * slots].reshape(count, cores, batches * slots, ada_cols), axis=1
    ).reshape(-1, ada_cols)
    g_ada_b = jnp.sum(d_modul, axis=0)
    g_ada = lax.dot_general(
        cond_all.reshape(-1, width).astype(F32),
        d_modul,
        (((0,), (0,)), ((), ())),
        precision=HIGHEST,
    )
    g_ada = lax.all_to_all(g_ada.reshape(devices, rows, ada_cols), both, 0, 0)
    g_ada = g_ada.swapaxes(0, 1).reshape(rows, 6 * width)

    s_att = jnp.concatenate([s_qkv, s_out], axis=1).reshape(cores, rows, -1)
    s_mine = lax.dynamic_index_in_dim(s_att, core, 0, keepdims=False)
    s_theirs = swap(lax.dynamic_index_in_dim(s_att, 1 - core, 0, keepdims=False))
    s_first = jnp.where(core == 0, s_mine, s_theirs)
    s_second = jnp.where(core == 0, s_theirs, s_mine)
    s_both = jnp.stack([s_first, s_second], axis=1)
    g_qkv = (
        s_both[:, :, : 3 * inner].reshape(rows, cores, 3, inner).swapaxes(1, 2).reshape(rows, -1)
    )
    g_out = s_both[:, :, 3 * inner :].reshape(rows, width)

    def tokens(x):
        return x.reshape(batches, 1, half, width)

    return (
        tokens(result),
        tokens(d_input),
        g_ada,
        g_ada_b,
        g_qkv,
        g_qkv_b,
        g_out,
        g_out_b,
        s_gate_up[:, :hidden],
        s_gate_up[:, hidden:],
        s_down.T,
    )


def shards_fast(
    hidden_in,
    cond_vec,
    seg_ids,
    grid_pos,
    out_grad,
    w_ada,
    b_ada,
    w_qkv,
    b_qkv,
    w_out,
    b_out,
    w_gate,
    w_up,
    w_down,
):
    count = lax.axis_size("wide")
    cores = lax.axis_size("narrow")
    devices = count * cores
    core = lax.axis_index("narrow")
    batches, _, half, width = hidden_in.shape
    slots = cond_vec.shape[2]
    own = batches * half
    heads = HEADS // cores
    inner = heads * HEAD
    rows = w_qkv.shape[0]
    both = ("wide", "narrow")

    qkv_cols = (3 * inner + 127) // 128 * 128
    out_cols = (width // cores + 127) // 128 * 128
    gap = width - out_cols
    heads_of = w_qkv.reshape(rows, 3, cores, inner).swapaxes(1, 2).reshape(rows, cores, 3 * inner)
    heads_of = jnp.pad(heads_of, ((0, 0), (0, 0), (0, qkv_cols - 3 * inner)))
    outs_of = jnp.stack([w_out[:, gap * c : gap * c + out_cols] for c in range(cores)], axis=1)
    by_half = jnp.concatenate([heads_of, outs_of], axis=2)
    mine = lax.dynamic_index_in_dim(by_half, core, 1, keepdims=False)
    theirs = lax.dynamic_index_in_dim(by_half, 1 - core, 1, keepdims=False)
    att = by_core(mine, swap(theirs), core, 0)
    hidden = w_gate.shape[1]
    down_t = w_down.T

    n_b = b_qkv.shape[0]
    b_own = jnp.concatenate([b_qkv, b_out])
    b_two = by_core(b_own[None], swap(b_own[None]), core, 0).reshape(1, -1)
    cond = jax.nn.silu(cond_vec[:, 0].astype(F32)).astype(BF16).reshape(batches * slots, width)
    told = jnp.concatenate([cond, jnp.pad(b_two, ((0, 0), (0, width - b_two.shape[1])))], axis=0)
    told = jnp.broadcast_to(told[None], (count,) + told.shape)
    told = lax.all_to_all(told, "wide", 0, 0)
    cond_all = told[:, : batches * slots]
    biases = told[:, batches * slots, : b_two.shape[1]].reshape(devices, -1)
    qkv_b = biases[:, :n_b].reshape(3, cores, inner).astype(F32)
    qkv_b = lax.dynamic_index_in_dim(qkv_b, core, 1, keepdims=False).reshape(-1)
    qkv_b = jnp.pad(qkv_b, (0, qkv_cols - 3 * inner))
    out_b = biases[:, n_b:].reshape(-1).astype(F32)

    ada_cols = w_ada.shape[1] // devices
    ada = lax.all_to_all(
        w_ada.reshape(rows, devices, ada_cols).swapaxes(0, 1), both, 0, 0
    ).reshape(devices * rows, ada_cols)
    modul = dot(cond_all.reshape(-1, width), ada) + b_ada.astype(F32)
    modul = modul.reshape(count, 1, batches * slots, ada_cols)
    modul = jnp.broadcast_to(modul, (count, cores, batches * slots, ada_cols))
    modul = lax.all_to_all(
        modul.reshape(devices, batches * slots, ada_cols), both, 0, 0
    )
    modul = modul.swapaxes(0, 1).reshape(batches * slots, 6 * width)

    segs = seg_ids[:, 0].reshape(batches, cores, half)
    seg_own = lax.dynamic_index_in_dim(segs, core, 1, keepdims=False)
    seg_other = lax.dynamic_index_in_dim(segs, 1 - core, 1, keepdims=False)
    seg_two = jnp.stack([seg_own, seg_other])
    seg_row = seg_two.swapaxes(0, 1).reshape(batches, 1, cores * half)
    slot_ids = seg_own + slots * jnp.arange(batches)[:, None]
    places = jnp.stack([grid_pos[0, :, 0], grid_pos[1, :, 0]]).reshape(2, own)
    places = jnp.stack([places, swap(places)], axis=1).reshape(2, 2 * own)
    cos, sin = turn_tables(places[0], places[1])

    x_own = hidden_in.reshape(own, width)
    dy_own = out_grad.reshape(own, width)
    slot_ids = slot_ids.reshape(own, 1)
    seg_col = seg_two.reshape(2 * own, 1)
    (
        qkv_w, out_w, gate_all, up_all, down_all, a_low, d_mlp_low, b1, b2, lse, o_heads, branch,
        mixed, c_low, hid, active, slope,
    ) = forward_call(
        x_own, dy_own, modul, slot_ids, seg_col, seg_row, cos, sin, qkv_b[None], out_b[None],
        att, w_gate, w_up, down_t, heads,
    )
    (
        result, d_input, s_gate, s_up, s_down, s_qkv, s_out, d_modul, g_qk_b, g_v_b, g_out_b,
    ) = backward_call(
        modul, slot_ids, seg_col, seg_row, cos, sin, lse, x_own, dy_own, branch, mixed, hid, active,
        slope, c_low, d_mlp_low, a_low, b1, b2, o_heads, gate_all.reshape(width, hidden),
        up_all.reshape(width, hidden), down_all.reshape(width, hidden), qkv_w, out_w, heads, out_cols,
    )
    g_qkv_b = jnp.concatenate([g_qk_b, g_v_b[:, :inner]], axis=1)
    g_out_b = g_out_b[0]
    s_out = jnp.where(core == 0, s_out[:, : width // cores], s_out[:, out_cols - width // cores :])
    d_modul = d_modul.reshape(batches * slots, devices, ada_cols).swapaxes(0, 1)
    b_parts = jnp.zeros((3, cores, inner), F32)
    b_parts = lax.dynamic_update_index_in_dim(b_parts, g_qkv_b.reshape(3, 1, inner), core, 1)
    bias_part = jnp.concatenate(
        [b_parts.reshape(devices, -1), g_out_b.reshape(devices, -1)], axis=1
    )
    n_bias = bias_part.shape[1]
    bias_rows = -(-n_bias // ada_cols)
    bias_part = jnp.pad(bias_part, ((0, 0), (0, bias_rows * ada_cols - n_bias)))
    message = jnp.concatenate(
        [d_modul, bias_part.reshape(devices, bias_rows, ada_cols)], axis=1
    )
    message = lax.all_to_all(message, both, 0, 0)
    g_bias = jnp.sum(message[:, batches * slots :], axis=0).reshape(-1)
    g_qkv_b, g_out_b = g_bias[:n_b], g_bias[n_b:n_bias]
    d_modul = jnp.sum(
        message[:, : batches * slots].reshape(count, cores, batches * slots, ada_cols), axis=1
    ).reshape(-1, ada_cols)
    g_ada_b = jnp.sum(d_modul, axis=0)
    g_ada = lax.dot_general(
        cond_all.reshape(-1, width).astype(F32),
        d_modul,
        (((0,), (0,)), ((), ())),
        precision=HIGHEST,
    )
    g_ada = lax.all_to_all(g_ada.reshape(devices, rows, ada_cols), both, 0, 0)
    g_ada = g_ada.swapaxes(0, 1).reshape(rows, 6 * width)

    s_att = jnp.concatenate([s_qkv[:, : 3 * inner], s_out], axis=1).reshape(cores, rows, -1)
    s_mine = lax.dynamic_index_in_dim(s_att, core, 0, keepdims=False)
    s_theirs = swap(lax.dynamic_index_in_dim(s_att, 1 - core, 0, keepdims=False))
    s_first = jnp.where(core == 0, s_mine, s_theirs)
    s_second = jnp.where(core == 0, s_theirs, s_mine)
    s_both = jnp.stack([s_first, s_second], axis=1)
    g_qkv = (
        s_both[:, :, : 3 * inner].reshape(rows, cores, 3, inner).swapaxes(1, 2).reshape(rows, -1)
    )
    g_out = s_both[:, :, 3 * inner :].reshape(rows, width)

    def tokens(x):
        return x.reshape(batches, 1, half, width)

    return (
        tokens(result),
        tokens(d_input),
        g_ada,
        g_ada_b,
        g_qkv,
        g_qkv_b,
        g_out,
        g_out_b,
        s_gate,
        s_up,
        s_down.T,
    )


def solution(mesh):
    both = ("wide", "narrow")
    in_specs = (
        P(None, "wide", "narrow", None),
        P(None, "wide", None, None),
        P(None, "wide", None),
        P(None, None, "wide", "narrow"),
        P(None, "wide", "narrow", None),
        P(both, None),
        P(both),
        P(both, None),
        P(both),
        P(both, None),
        P(both),
        P("wide", "narrow"),
        P("wide", "narrow"),
        P("narrow", "wide"),
    )
    out_specs = (
        P(None, "wide", "narrow", None),
        P(None, "wide", "narrow", None),
        P(both, None),
        P(both),
        P(both, None),
        P(both),
        P(both, None),
        P(both),
        P("wide", "narrow"),
        P("wide", "narrow"),
        P("narrow", "wide"),
    )
    shards = shards_fast if mesh.shape["wide"] == 16 else shards_any
    return jax.shard_map(shards, mesh=mesh, in_specs=in_specs, out_specs=out_specs, check_vma=False)
```
